256 devices in a mesh: seq: 64 (over x, z_hi, y, core), tp: 4 (over z_lo).
Axes of the slice: x: 4, y: 4, z: 8 (z_hi: 2, z_lo: 4; z = z_hi * 4 + z_lo), core: 2. Of those that a mesh axis runs over, the one named last changes fastest.
Arguments:
- projected: float32 [3, 32768, 4096], P(None, 'seq', 'tp'), may hold values from -6 to 6
- short_filter: float32 [3, 7, 4096], P(None, None, 'tp'), may hold values from -2 to 2
- long_filter: float32 [4, 32768], P(None, ('seq', 'tp')), may hold values from -0.03125 to 0.03125
- skip_gain: float32 [4096], P('tp'), may hold values from 0.1 to 1.9
Outputs:
- mixed: float32 [32768, 4096], P('seq', 'tp')
The draws below stay inside these ranges and needn't reach their ends.
All inputs are finite; a program needn't handle non-finite values.
Results may differ from the reference program's by a relative error of at most 0.000098.
Values sent between devices are 32-bit elements; how exact they have to be, the bound alone decides.
No kernel may reach another device: no remote copies, remote signals or barrier semaphores. Data moves between devices by JAX's collectives and lax.ppermute only.
A program may use at most 128 MiB of HBM per device.

```python
import jax
import jax.numpy as jnp
from jax import lax

D = 4096
GROUPS = 4
SHORT = 7
LEN = 32768


def level_of(own_key, shape, cuts, least, largest):
    level = 1.0
    for axis_at, blocks in cuts:
        steps = jax.random.uniform(jax.random.fold_in(jax.random.fold_in(own_key, 6), axis_at), (blocks,), jnp.float32, least / len(cuts), largest / len(cuts))
        level = level * jnp.repeat(jnp.exp(steps), shape[axis_at] // blocks).reshape((-1,) + (1,) * (len(shape) - 1 - axis_at))
    return level


def noise(key, extent, scale, reach, pieces=(), held_as=jnp.bfloat16):
    array = scale * jax.random.normal(key, extent, jnp.float32)
    if pieces:
        array = array * level_of(key, extent, pieces, -0.22, 0.18)
    return jnp.clip(array, -reach, reach).astype(held_as)


def setup_inputs(seed: int = 0) -> dict:
    key_list = jax.random.split(jax.random.key(seed), 5)
    projected = noise(key_list[0], (3, LEN, D), 1.0, 6.0, ((1, 64), (2, 4)), jnp.float32)
    short_filter = noise(key_list[1], (3, SHORT, D), SHORT ** -0.5, 2.0, ((2, 4),), jnp.float32)
    long_filter = noise(key_list[2], (GROUPS, LEN), LEN ** -0.5, 0.03125, ((1, 256),), jnp.float32)
    skip_gain = jnp.clip(1.0 + 0.18 * jax.random.normal(key_list[3], (D,), jnp.float32), 0.1, 1.9)
    return dict(projected=projected, short_filter=short_filter, long_filter=long_filter, skip_gain=skip_gain)


def reference(projected, short_filter, long_filter, skip_gain):
    length = projected.shape[1]
    padded = jnp.concatenate([jnp.zeros((3, SHORT - 1, D), jnp.float32), projected], axis=1)
    features = short_filter[:, 0:1, :] * padded[:, 0:length, :]
    for offset in range(1, SHORT):
        features = features + short_filter[:, offset:offset + 1, :] * padded[:, offset:offset + length, :]
    gate_rows = features[0]
    product = features[1] * features[2]
    group_width = D // GROUPS
    spectra = jnp.fft.rfft(long_filter, n=2 * length, axis=1)

    def one_group(group_index):
        columns_block = lax.dynamic_slice_in_dim(product, group_index * group_width, group_width, 1)
        series_spec = jnp.fft.rfft(columns_block, n=2 * length, axis=0)
        taps_spec = lax.dynamic_slice_in_dim(spectra, group_index, 1, 0)[0]
        return jnp.fft.irfft(series_spec * taps_spec[:, None], n=2 * length, axis=0)[:length]

    stacked = lax.map(one_group, jnp.arange(GROUPS, dtype=jnp.int32))
    long_out = jnp.transpose(stacked, (1, 0, 2)).reshape(length, D)
    return gate_rows * (long_out + skip_gain * product)
```

```python
import functools

import jax
import jax.numpy as jnp
import ml_dtypes
import numpy as np
from jax import lax
from jax.experimental import pallas as pl
from jax.experimental.pallas import tpu as pltpu
from jax.sharding import Mesh
from jax.sharding import PartitionSpec as P

f32 = jnp.float32
bf16 = jnp.bfloat16

ROWS = 512
TAPS = 7
LANES = 128
PEERS = 32
PIECE = 8
QUARTERS = ROWS // LANES
BLOCK = QUARTERS * PIECE
HALF = PEERS * BLOCK
LENGTH = 32768
VMEM_BYTES = 60 << 20
ORDER = 256

SEQ = ("x", "zh", "y", "core")
PLANE = ("x", "y", "core")


def split_np(table):
    high = table.astype(np.float32).astype(ml_dtypes.bfloat16)
    low = (table - high.astype(np.float64)).astype(ml_dtypes.bfloat16)
    return high, low


def position_blocks():
    n1 = np.zeros((2, 4, PEERS), np.int64)
    for z in range(2):
        for q in range(4):
            for p in range(PEERS):
                x, rest = divmod(p, 8)
                n1[z, q, p] = 4 * (x * 16 + z * 8 + rest) + q
    return n1.reshape(-1)


def make_tables():
    n1 = position_blocks()
    k1 = np.arange(ORDER)
    m = np.arange(LANES)
    turn = 2.0 * np.pi
    first = turn * (((4 * k1[:, None] + 1) * n1[None, :]) % (4 * ORDER)) / (4 * ORDER)
    first = np.concatenate([np.cos(first), -np.sin(first)], axis=0)
    bend = turn * ((4 * k1[:, None] + 1) * m[None, :]) / (4 * LENGTH)
    second = turn * ((m[:, None] * m[None, :]) % LANES) / LANES
    cosine, sine = np.cos(second), np.sin(second)
    onward = np.block([[cosine, -sine], [sine, cosine]])
    back = np.block([[cosine, sine], [-sine, cosine]])
    last = first.T
    first_high, first_low = split_np(first)
    onward_high, onward_low = split_np(onward)
    back_high, back_low = split_np(back)
    last_high, last_low = split_np(last)
    return dict(
        first=np.concatenate([first_high, first_high, first_low], axis=1),
        last=np.concatenate([last_high, last_high, last_low], axis=1),
        onward=np.concatenate([onward_high, onward_high, onward_low], axis=0),
        back=np.concatenate([back_high, back_high, back_low], axis=0),
        bend=np.stack([np.cos(bend), -np.sin(bend)]).astype(np.float32),
    )


def halves(x):
    high = x.astype(bf16)
    low = (x - high.astype(f32)).astype(bf16)
    return high, low


def dot(a, b):
    return jnp.dot(a, b, preferred_element_type=f32)


def to_spectrum(columns, first, onward, bend):
    high, low = halves(columns)
    section = dot(first, jnp.concatenate([high, low, high], axis=0))
    bend_re, bend_im = bend[0], bend[1]
    rows = []
    for at in range(columns.shape[1] // LANES):
        re = section[:ORDER, at * LANES : (at + 1) * LANES]
        im = section[ORDER:, at * LANES : (at + 1) * LANES]
        rows.append(
            jnp.concatenate([re * bend_re - im * bend_im, re * bend_im + im * bend_re], axis=1)
        )
    bent = jnp.concatenate(rows, axis=0)
    high, low = halves(bent)
    return dot(jnp.concatenate([high, low, high], axis=1), onward)


def from_spectrum(spectrum, last, back, bend):
    high, low = halves(spectrum)
    section = dot(jnp.concatenate([high, low, high], axis=1), back)
    bend_re, bend_im = bend[0], bend[1]
    columns = []
    for at in range(spectrum.shape[0] // ORDER):
        re = section[at * ORDER : (at + 1) * ORDER, :LANES]
        im = section[at * ORDER : (at + 1) * ORDER, LANES:]
        columns.append(
            jnp.concatenate([re * bend_re + im * bend_im, im * bend_re - re * bend_im], axis=0)
        )
    bent = jnp.concatenate(columns, axis=1)
    high, low = halves(bent)
    return dot(last, jnp.concatenate([high, low, high], axis=0))


def conv_kernel(
    layout,
    sources,
    z_ref,
    *refs,
):
    own_ref, other_ref, spectrum_ref = (refs[:sources] * 3)[:3]
    first_ref, last_ref, onward_ref, back_ref, bend_ref = refs[sources : sources + 5]
    out_refs = refs[sources + 5 :]
    own_at, own_stride, other_at, other_stride, taps_at = layout
    low_plane = z_ref[0] == 0
    bend = bend_ref[...]
    if taps_at is not None:
        pieces = [spectrum_ref[pl.ds(taps_at + zq, PEERS, stride=own_stride), :] for zq in range(8)]
        taps = to_spectrum(jnp.concatenate(pieces, axis=0), first_ref[...], onward_ref[...], bend)
        taps = taps * (1.0 / LENGTH)
        out_refs[2][...] = taps
    else:
        taps = spectrum_ref[...]
    taps_re = taps[:, :LANES]
    taps_im = taps[:, LANES:]
    for pair in range(PIECE // 2):
        columns = []
        for channel in (2 * pair, 2 * pair + 1):
            own, other = [], []
            for q in range(4):
                row = q * PIECE + channel
                own.append(own_ref[pl.ds(own_at + row, PEERS, stride=own_stride), :])
                other.append(other_ref[pl.ds(other_at + row, PEERS, stride=other_stride), :])
            own = jnp.concatenate(own, axis=0)
            other = jnp.concatenate(other, axis=0)
            columns.append(
                jnp.concatenate(
                    [jnp.where(low_plane, own, other), jnp.where(low_plane, other, own)], axis=0
                )
            )
        spectrum = to_spectrum(
            jnp.concatenate(columns, axis=1), first_ref[...], onward_ref[...], bend
        )
        rows = []
        for at in range(2):
            re = spectrum[at * ORDER : (at + 1) * ORDER, :LANES]
            im = spectrum[at * ORDER : (at + 1) * ORDER, LANES:]
            rows.append(
                jnp.concatenate([re * taps_re - im * taps_im, re * taps_im + im * taps_re], axis=1)
            )
        result = from_spectrum(
            jnp.concatenate(rows, axis=0), last_ref[...], back_ref[...], bend
        )
        for at, channel in enumerate((2 * pair, 2 * pair + 1)):
            upper = result[: ORDER // 2, at * LANES : (at + 1) * LANES]
            lower = result[ORDER // 2 :, at * LANES : (at + 1) * LANES]
            own = jnp.where(low_plane, upper, lower)
            other = jnp.where(low_plane, lower, upper)
            for q in range(4):
                row = q * PIECE + channel
                rows_own = own[q * PEERS : (q + 1) * PEERS]
                rows_other = other[q * PEERS : (q + 1) * PEERS]
                if len(out_refs) == 1:
                    out_refs[0][pl.ds(row, PEERS, stride=2 * BLOCK), :] = rows_own
                    out_refs[0][pl.ds(BLOCK + row, PEERS, stride=2 * BLOCK), :] = rows_other
                else:
                    out_refs[0][pl.ds(row, PEERS, stride=BLOCK), :] = rows_own
                    out_refs[1][pl.ds(row, PEERS, stride=BLOCK), :] = rows_other


def feature_kernel(
    z_ref, proj_ref, halo_ref, short_ref, skip_ref, sent_ref, gate_ref, direct_ref, long_ref
):
    step = 64
    for j in range(3):
        long_ref[j, 0:8, :] = halo_ref[j]
        long_ref[j, 8 : ROWS + 8, :] = proj_ref[j]
    skip = skip_ref[0:1, :]
    for start in range(0, ROWS, LANES):
        parts = []
        for at in range(start, start + LANES, step):
            features = []
            for j in range(3):
                total = short_ref[j, 0:1, :] * long_ref[j, at + 2 : at + 2 + step, :]
                for i in range(1, TAPS):
                    total = total + short_ref[j, i : i + 1, :] * long_ref[
                        j, at + 2 + i : at + 2 + i + step, :
                    ]
                features.append(total)
            product = features[1] * features[2]
            gate_ref[at : at + step, :] = features[0]
            direct_ref[at : at + step, :] = features[0] * (skip * product)
            parts.append(product)
        turned = jnp.concatenate(parts, axis=0).T
        sent_ref[:, start // LANES] = turned.reshape(LANES // PIECE, PIECE, LANES)


def final_kernel(z_ref, long_ref, gate_ref, direct_ref, *rest):
    out_ref = rest[-1]
    for start in range(0, ROWS, LANES):
        turned = long_ref[:, start // LANES].reshape(LANES, LANES).T
        out_ref[start : start + LANES, :] = (
            gate_ref[start : start + LANES, :] * turned + direct_ref[start : start + LANES, :]
        )


def block_of(z, slot, half, chunk):
    plane = z if slot == 0 else 1 - z
    return chunk * 4 + plane * 2 + half


def features_of(z, chunk, slots, projected, halo, short_filter, skip):
    count = len(slots)

    def column(i, z_ref):
        plane = z_ref[0]
        if slots == (1,):
            plane = 1 - plane
        elif count == 2:
            plane = jnp.where(i // 2 == 0, plane, 1 - plane)
        return chunk * 4 + plane * 2 + i % 2

    blocks = 2 * count
    return pl.pallas_call(
        feature_kernel,
        grid_spec=pltpu.PrefetchScalarGridSpec(
            num_scalar_prefetch=1,
            grid=(blocks,),
            in_specs=[
                pl.BlockSpec((3, ROWS, LANES), lambda i, z: (0, 0, column(i, z))),
                pl.BlockSpec((3, 8, LANES), lambda i, z: (0, 0, column(i, z))),
                pl.BlockSpec((3, TAPS, LANES), lambda i, z: (0, 0, column(i, z))),
                pl.BlockSpec((1, LANES), lambda i, z: (0, column(i, z))),
            ],
            out_specs=[
                pl.BlockSpec(
                    (LANES // PIECE, None, QUARTERS, PIECE, LANES),
                    lambda i, z: (i % 2, i // 2, 0, 0, 0),
                ),
                pl.BlockSpec((ROWS, LANES), lambda i, z: (0, i)),
                pl.BlockSpec((ROWS, LANES), lambda i, z: (0, i)),
            ],
            scratch_shapes=[pltpu.VMEM((3, ROWS + 8, LANES), f32)],
        ),
        out_shape=[
            jax.ShapeDtypeStruct((PEERS, count, QUARTERS, PIECE, LANES), f32),
            jax.ShapeDtypeStruct((ROWS, blocks * LANES), f32),
            jax.ShapeDtypeStruct((ROWS, blocks * LANES), f32),
        ],
        compiler_params=pltpu.CompilerParams(vmem_limit_bytes=VMEM_BYTES),
        cost_estimate=pl.CostEstimate(
            flops=blocks * 6_000_000, bytes_accessed=blocks * 1_600_000, transcendentals=0
        ),
        name="features",
    )(z, projected, halo, short_filter, skip)


def finish(z, chunk, slots, long_out, in_slot, gate, direct, gate_at, whole):
    count = len(slots)

    def column(i, z_ref):
        plane = z_ref[0]
        if slots == (1,):
            plane = 1 - plane
        elif count == 2:
            plane = jnp.where(i // 2 == 0, plane, 1 - plane)
        return chunk * 4 + plane * 2 + i % 2

    operands = [z, long_out, gate, direct]
    in_specs = [
        pl.BlockSpec(
            (LANES // PIECE, None, QUARTERS, PIECE, LANES),
            lambda i, z: (i % 2, in_slot + i // 2, 0, 0, 0),
        ),
        pl.BlockSpec((ROWS, LANES), lambda i, z: (0, gate_at + i)),
        pl.BlockSpec((ROWS, LANES), lambda i, z: (0, gate_at + i)),
    ]
    aliases = {}
    if whole is not None:
        aliases = {len(operands): 0}
        operands.append(whole)
        in_specs.append(pl.BlockSpec(memory_space=pl.ANY))
    return pl.pallas_call(
        final_kernel,
        grid_spec=pltpu.PrefetchScalarGridSpec(
            num_scalar_prefetch=1,
            grid=(2 * count,),
            in_specs=in_specs,
            out_specs=pl.BlockSpec((ROWS, LANES), lambda i, z: (0, column(i, z))),
        ),
        out_shape=jax.ShapeDtypeStruct((ROWS, 8 * LANES), f32),
        input_output_aliases=aliases,
        compiler_params=pltpu.CompilerParams(vmem_limit_bytes=VMEM_BYTES),
        cost_estimate=pl.CostEstimate(
            flops=count * 300_000, bytes_accessed=count * 2_100_000, transcendentals=0
        ),
        name="finish",
    )(*operands)


def convolve(z, layout, sources, tables, joined):
    if joined:
        out_shape = [jax.ShapeDtypeStruct((2 * HALF, LANES), f32)]
    else:
        out_shape = [jax.ShapeDtypeStruct((HALF, LANES), f32)] * 2
        out_shape = out_shape + [jax.ShapeDtypeStruct((ORDER, 2 * LANES), f32)]
    operands = list(sources) + [
        tables[name] for name in ("first", "last", "onward", "back", "bend")
    ]
    return pl.pallas_call(
        functools.partial(conv_kernel, layout, len(sources)),
        grid_spec=pltpu.PrefetchScalarGridSpec(
            num_scalar_prefetch=1,
            grid=(1,),
            in_specs=[whole_spec(x.shape) for x in operands],
            out_specs=[whole_spec(x.shape) for x in out_shape],
        ),
        out_shape=out_shape,
        compiler_params=pltpu.CompilerParams(vmem_limit_bytes=VMEM_BYTES),
        cost_estimate=pl.CostEstimate(
            flops=3_300_000_000, bytes_accessed=5_000_000, transcendentals=0
        ),
        name="convolve",
    )(z, *operands)


def whole_spec(shape):
    return pl.BlockSpec(shape, lambda i, z: (0,) * len(shape))


def swap_planes(x):
    return lax.ppermute(x, "zh", [(0, 1), (1, 0)])


def across(x):
    return lax.all_to_all(x, PLANE, split_axis=0, concat_axis=0, tiled=True)


def body(projected, short_filter, long_filter, skip_gain):
    tables = {name: jnp.asarray(table) for name, table in make_tables().items()}
    z = lax.axis_index("zh").astype(jnp.int32).reshape(1)
    skip = skip_gain.reshape(1, -1)
    devices = lax.axis_size(SEQ)
    halo = lax.ppermute(
        projected[:, ROWS - 8 :, :], SEQ, [(i, i + 1) for i in range(devices - 1)]
    )
    feature = functools.partial(
        features_of, projected=projected, halo=halo, short_filter=short_filter, skip=skip
    )
    a_other, gate_ao, direct_ao = feature(z, 0, (1,))
    a_from = swap_planes(a_other)
    z1, _ = lax.optimization_barrier((z, a_other))
    b_both, gate_b, direct_b = feature(z1, 1, (0, 1))
    b_here = across(b_both)
    z2, _ = lax.optimization_barrier((z, a_other))
    a_own, gate_a, direct_a = feature(z2, 0, (0,))

    pieces, _ = lax.optimization_barrier((long_filter, a_other))
    pieces = jnp.concatenate([pieces, pieces], axis=0)
    taps = lax.all_to_all(pieces, ("zh", "zl"), split_axis=0, concat_axis=0, tiled=True)

    a_from, b_here, taps = lax.optimization_barrier((a_from, b_here, taps))
    b_from = swap_planes(b_here[:, 1])
    a_here = across(
        jnp.concatenate(
            [
                a_own.reshape(PEERS, BLOCK, LANES),
                a_from.reshape(PEERS, BLOCK, LANES),
                jnp.broadcast_to(taps[None], (PEERS, 8, LANES)),
            ],
            axis=1,
        )
    )
    a_flat = a_here.reshape(-1, LANES)
    wide = 2 * BLOCK + 8
    conv_a_own, conv_a_other, spectrum = convolve(
        z, (0, wide, BLOCK, wide, 2 * BLOCK), (a_flat,), tables, False
    )
    a_back = swap_planes(conv_a_other)
    z3, _ = lax.optimization_barrier((z, conv_a_other))
    (conv_b,) = convolve(
        z3,
        (0, 2 * BLOCK, 0, BLOCK, None),
        (b_here.reshape(2 * HALF, LANES), b_from.reshape(HALF, LANES), spectrum),
        tables,
        True,
    )
    b_out = across(conv_b.reshape(PEERS, 2, QUARTERS, PIECE, LANES))
    a_back, b_out = lax.optimization_barrier((a_back, b_out))
    b_back = swap_planes(b_out[:, 1])
    a_out = across(
        jnp.stack([conv_a_own, a_back], 0)
        .reshape(2, PEERS, QUARTERS, PIECE, LANES)
        .transpose(1, 0, 2, 3, 4)
    )
    mixed = finish(z, 1, (0,), b_out, 0, gate_b, direct_b, 0, None)
    mixed = finish(z, 0, (0,), a_out, 0, gate_a, direct_a, 0, mixed)
    mixed = finish(z, 0, (1,), a_out, 1, gate_ao, direct_ao, 0, mixed)
    mixed = finish(z, 1, (1,), b_back[:, None], 0, gate_b, direct_b, 2, mixed)
    return mixed


def solution(mesh):
    fine = Mesh(mesh.devices.reshape(4, 2, 4, 2, 4), ("x", "zh", "y", "core", "zl"))
    placed = (P(None, SEQ, "zl"), P(None, None, "zl"), P(None, SEQ + ("zl",)), P("zl"))
    return jax.shard_map(
        body, mesh=fine, in_specs=placed, out_specs=P(SEQ, "zl"), check_vma=False
    )
```

```python
import functools

import jax
import jax.numpy as jnp
import ml_dtypes
import numpy as np
from jax import lax
from jax.experimental import pallas as pl
from jax.experimental.pallas import tpu as pltpu
from jax.sharding import Mesh
from jax.sharding import PartitionSpec as P

f32 = jnp.float32
bf16 = jnp.bfloat16

ROWS = 512
TAPS = 7
LANES = 128
PEERS = 32
PIECE = 8
QUARTERS = ROWS // LANES
BLOCK = QUARTERS * PIECE
HALF = PEERS * BLOCK
LENGTH = 32768
VMEM_BYTES = 16 << 20
CONV_BYTES = 40 << 20
SLOW = 200_000
ORDER = 256

SEQ = ("x", "zh", "y", "core")
PLANE = ("x", "y", "core")


def split_np(table):
    high = table.astype(np.float32).astype(ml_dtypes.bfloat16)
    low = (table - high.astype(np.float64)).astype(ml_dtypes.bfloat16)
    return high, low


def position_blocks():
    n1 = np.zeros((2, 4, PEERS), np.int64)
    for z in range(2):
        for q in range(4):
            for p in range(PEERS):
                x, rest = divmod(p, 8)
                n1[z, q, p] = 4 * (x * 16 + z * 8 + rest) + q
    return n1.reshape(-1)


def make_tables():
    n1 = position_blocks()
    k1 = np.arange(ORDER)
    m = np.arange(LANES)
    turn = 2.0 * np.pi
    first = turn * (((4 * k1[:, None] + 1) * n1[None, :]) % (4 * ORDER)) / (4 * ORDER)
    first = np.concatenate([np.cos(first), -np.sin(first)], axis=0)
    bend = turn * ((4 * k1[:, None] + 1) * m[None, :]) / (4 * LENGTH)
    second = turn * ((m[:, None] * m[None, :]) % LANES) / LANES
    cosine, sine = np.cos(second), np.sin(second)
    onward = np.block([[cosine, -sine], [sine, cosine]])
    back = np.block([[cosine, sine], [-sine, cosine]])
    last = first.T
    first_high, first_low = split_np(first)
    onward_high, onward_low = split_np(onward)
    back_high, back_low = split_np(back)
    last_high, last_low = split_np(last)
    return dict(
        first=np.concatenate([first_high, first_low], axis=1),
        last=np.concatenate([last_high, last_low], axis=1),
        onward=np.concatenate([onward_high, onward_low], axis=0),
        back=np.concatenate([back_high, back_low], axis=0),
        bend=np.stack([np.cos(bend), -np.sin(bend)]).astype(np.float32),
    )


def halves(x):
    high = x.astype(bf16)
    low = (x - high.astype(f32)).astype(bf16)
    return high, low


def thrice(table, axis):
    half = table.shape[axis] // 2
    high = lax.slice_in_dim(table, 0, half, axis=axis)
    return jnp.concatenate([high, table], axis=axis)


def dot(a, b):
    return jnp.dot(a, b, preferred_element_type=f32)


def to_spectrum(columns, first, onward, bend):
    high, low = halves(columns)
    section = dot(first, jnp.concatenate([high, low, high], axis=0))
    bend_re, bend_im = bend[0], bend[1]
    rows = []
    for at in range(columns.shape[1] // LANES):
        re = section[:ORDER, at * LANES : (at + 1) * LANES]
        im = section[ORDER:, at * LANES : (at + 1) * LANES]
        rows.append(
            jnp.concatenate([re * bend_re - im * bend_im, re * bend_im + im * bend_re], axis=1)
        )
    bent = jnp.concatenate(rows, axis=0)
    high, low = halves(bent)
    return dot(jnp.concatenate([high, low, high], axis=1), onward)


def from_spectrum(spectrum, last, back, bend):
    high, low = halves(spectrum)
    section = dot(jnp.concatenate([high, low, high], axis=1), back)
    bend_re, bend_im = bend[0], bend[1]
    columns = []
    for at in range(spectrum.shape[0] // ORDER):
        re = section[at * ORDER : (at + 1) * ORDER, :LANES]
        im = section[at * ORDER : (at + 1) * ORDER, LANES:]
        columns.append(
            jnp.concatenate([re * bend_re + im * bend_im, im * bend_re - re * bend_im], axis=0)
        )
    bent = jnp.concatenate(columns, axis=1)
    high, low = halves(bent)
    return dot(last, jnp.concatenate([high, low, high], axis=0))


def pieces_of(source_ref, target_ref, count):
    count = min(count, source_ref.shape[0])
    rows = source_ref.shape[0] // count
    cuts = [pl.ds(at * rows, rows) for at in range(count)]
    return [(source_ref.at[cut], target_ref.at[cut]) for cut in cuts]


def copies_of(pairs, sems):
    copies = [
        pltpu.make_async_copy(source, target, sems.at[at])
        for at, (source, target) in enumerate(pairs)
    ]
    for copy in copies:
        copy.start()
    return copies


def wait_all(copies):
    for copy in copies:
        copy.wait()


CUTS = 1


BATCH = 2
LAG = 1


def pieces_taps(ref, at, stride):
    return jnp.concatenate([ref[pl.ds(at + zq, PEERS, stride=stride), :] for zq in range(8)], axis=0)


def conv_kernel(layout, sources, outputs, after, z_ref, *refs):
    own_at, own_stride, other_at, other_stride, taps_at = layout
    inputs = sources + 5
    given, results = refs[:inputs], refs[inputs + after : inputs + after + outputs]
    held = refs[inputs + after + outputs : -2]
    in_sems, out_sems = refs[-2:]
    order = list(range(sources)) + [sources + at for at in (0, 4, 2, 3, 1)]
    arrivals = {}
    for k in order:
        arrivals[k] = copies_of(pieces_of(given[k], held[k], CUTS), in_sems.at[k])
    own_ref, other_ref, spectrum_ref = (held[:sources] * 3)[:3]
    first_ref, last_ref, onward_ref, back_ref, bend_ref = held[sources:inputs]
    out_refs = held[inputs:]
    low_plane = z_ref[0] == 0
    wide = 2 * BLOCK if outputs == 1 else BLOCK

    for k in range(sources):
        wait_all(arrivals[k])
    extra = [pieces_taps(spectrum_ref, taps_at, own_stride)] if taps_at is not None else []
    wait_all(arrivals[sources] + arrivals[sources + 4] + arrivals[sources + 2])
    bend = bend_ref[...]
    bend_re, bend_im = bend[0], bend[1]
    leaving = []
    if taps_at is not None:
        taps = to_spectrum(extra[0], thrice(first_ref[...], 1), thrice(onward_ref[...], 0), bend) * (1.0 / LENGTH)
        out_refs[2][...] = taps
        leaving = copies_of(pieces_of(out_refs[2], results[2], 1), out_sems.at[2])
    else:
        taps = spectrum_ref[...]
    taps_re = taps[:, :LANES]
    taps_im = taps[:, LANES:]

    def gather(at):
        own, other = [], []
        for q in range(4):
            row = q * PIECE + at
            own.append(own_ref[pl.ds(own_at + row, PEERS, stride=own_stride), :])
            other.append(other_ref[pl.ds(other_at + row, PEERS, stride=other_stride), :])
        own = jnp.concatenate(own, axis=0)
        other = jnp.concatenate(other, axis=0)
        return jnp.concatenate(
            [jnp.where(low_plane, own, other), jnp.where(low_plane, other, own)], axis=0
        )

    def store(at, column):
        upper, lower = column[: ORDER // 2], column[ORDER // 2 :]
        own = jnp.where(low_plane, upper, lower)
        other = jnp.where(low_plane, lower, upper)
        for q in range(4):
            row = q * PIECE + at
            rows_own = own[q * PEERS : (q + 1) * PEERS]
            rows_other = other[q * PEERS : (q + 1) * PEERS]
            out_refs[0][pl.ds(row, PEERS, stride=wide), :] = rows_own
            if outputs == 1:
                out_refs[0][pl.ds(BLOCK + row, PEERS, stride=2 * BLOCK), :] = rows_other
            else:
                out_refs[1][pl.ds(row, PEERS, stride=BLOCK), :] = rows_other

    def load(channels):
        high, low = halves(jnp.concatenate([gather(at) for at in channels], axis=1))
        return jnp.concatenate([high, low, high], axis=0)

    def to_blocks(x):
        return dot(thrice(first_ref[...], 1), x)

    def bend_onward(section):
        rows = []
        for at in range(section.shape[1] // LANES):
            re = section[:ORDER, at * LANES : (at + 1) * LANES]
            im = section[ORDER:, at * LANES : (at + 1) * LANES]
            rows.append(
                jnp.concatenate([re * bend_re - im * bend_im, re * bend_im + im * bend_re], axis=1)
            )
        high, low = halves(jnp.concatenate(rows, axis=0))
        return jnp.concatenate([high, low, high], axis=1)

    def to_frequencies(x):
        return dot(x, thrice(onward_ref[...], 0))

    def weigh(spectrum):
        rows = []
        for at in range(spectrum.shape[0] // ORDER):
            re = spectrum[at * ORDER : (at + 1) * ORDER, :LANES]
            im = spectrum[at * ORDER : (at + 1) * ORDER, LANES:]
            rows.append(
                jnp.concatenate([re * taps_re - im * taps_im, re * taps_im + im * taps_re], axis=1)
            )
        high, low = halves(jnp.concatenate(rows, axis=0))
        return jnp.concatenate([high, low, high], axis=1)

    def from_frequencies(x):
        return dot(x, thrice(back_ref[...], 0))

    def bend_back(section):
        columns = []
        for at in range(section.shape[0] // ORDER):
            re = section[at * ORDER : (at + 1) * ORDER, :LANES]
            im = section[at * ORDER : (at + 1) * ORDER, LANES:]
            columns.append(
                jnp.concatenate([re * bend_re + im * bend_im, im * bend_re - re * bend_im], axis=0)
            )
        high, low = halves(jnp.concatenate(columns, axis=1))
        return jnp.concatenate([high, low, high], axis=0)

    def from_blocks(x):
        return dot(thrice(last_ref[...], 1), x)

    stages = (
        load, to_blocks, bend_onward, to_frequencies, weigh, from_frequencies, bend_back, from_blocks
    )
    batches = [tuple(range(at, at + BATCH)) for at in range(0, PIECE, BATCH)]
    state = list(batches)
    for tick in range(len(stages) + 1 + LAG * (len(batches) - 1)):
        if tick == 5:
            wait_all(arrivals[sources + 3] + arrivals[sources + 1])
        for batch, channels in enumerate(batches):
            stage = tick - LAG * batch
            if 0 <= stage < len(stages):
                state[batch] = stages[stage](state[batch])
            elif stage == len(stages):
                for at, channel in enumerate(channels):
                    store(channel, state[batch][:, at * LANES : (at + 1) * LANES])
    for k in range(min(outputs, 2)):
        leaving = leaving + copies_of(pieces_of(out_refs[k], results[k], CUTS), out_sems.at[k])
    wait_all(leaving)


def short_sum(short, long_ref, at, step):
    total = short[0:1] * long_ref[at + 2 : at + 2 + step, :]
    for i in range(1, TAPS):
        total = total + short[i : i + 1] * long_ref[at + 2 + i : at + 2 + i + step, :]
    return total


def fetch(proj_ref, halo_ref, short_ref, buffer_ref, halo_held, taps_held, sems, streams, columns):
    edges = copies_of([(halo_ref, halo_held), (short_ref, taps_held)], sems.at[len(columns)])
    first, count = streams
    blocks = []
    for i, column in enumerate(columns):
        lanes = pl.ds(pl.multiple_of(column, LANES), LANES)
        copy = pltpu.make_async_copy(
            proj_ref.at[pl.ds(first, count), :, lanes],
            buffer_ref.at[i, :, pl.ds(8, ROWS)],
            sems.at[i, 0],
        )
        copy.start()
        blocks.append(copy)
    wait_all(edges)
    for i, column in enumerate(columns):
        lanes = pl.ds(pl.multiple_of(column, LANES), LANES)
        buffer_ref[i, :, 0:8, :] = halo_held[first : first + count, :, lanes]
    return blocks


def feature_kernel(columns_of_z, z_ref, halo_ref, short_ref, proj_ref, *rest):
    sent_ref, product_ref = rest[-9:-7]
    buffer_ref, halo_held, taps_held, sems, out_sems, turned_ref, flat_ref = rest[-7:]
    step = 64
    columns = columns_of_z(z_ref[0])
    blocks = fetch(
        proj_ref, halo_ref, short_ref, buffer_ref, halo_held, taps_held, sems, (1, 2), columns
    )
    peers = LANES // PIECE
    leaving = []
    for i, copy in enumerate(blocks):
        copy.wait()
        lanes = pl.ds(pl.multiple_of(columns[i], LANES), LANES)
        key_taps, value_taps = taps_held[1, :, lanes], taps_held[2, :, lanes]
        for quarter in range(QUARTERS):
            parts = []
            for at in range(quarter * LANES, (quarter + 1) * LANES, step):
                product = short_sum(key_taps, buffer_ref.at[i, 0], at, step) * short_sum(
                    value_taps, buffer_ref.at[i, 1], at, step
                )
                flat_ref[i, at : at + step, :] = product
                parts.append(product)
            turned = jnp.concatenate(parts, axis=0).T
            turned_ref[i, :, quarter] = turned.reshape(peers, PIECE, LANES)
        into = sent_ref.at[
            pl.ds(i % 2 * peers, peers), pl.ds(i // 2 * QUARTERS, QUARTERS)
        ]
        pairs = [(turned_ref.at[i], into)]
        pairs.append((flat_ref.at[i], product_ref.at[:, pl.ds(i * LANES, LANES)]))
        leaving = leaving + copies_of(pairs, out_sems.at[i])
    wait_all(leaving)


def gate_kernel(z_ref, halo_ref, short_ref, proj_ref, *rest):
    gate_ref, buffer_ref, halo_held, taps_held, sems, out_sems, flat_ref = rest[-7:]
    step = 64
    columns = [i * LANES for i in range(8)]
    blocks = fetch(
        proj_ref, halo_ref, short_ref, buffer_ref, halo_held, taps_held, sems, (0, 1), columns
    )
    leaving = []
    for i, copy in enumerate(blocks):
        copy.wait()
        taps = taps_held[0, :, i * LANES : (i + 1) * LANES]
        for at in range(0, ROWS, step):
            flat_ref[i, at : at + step, :] = short_sum(taps, buffer_ref.at[i, 0], at, step)
        pairs = [(flat_ref.at[i], gate_ref.at[:, pl.ds(i * LANES, LANES)])]
        leaving = leaving + copies_of(pairs, out_sems.at[i])
    wait_all(leaving)


def final_kernel(z_ref, long_ref, gate_ref, product_ref, skip_ref, *rest):
    out_ref = rest[-1]
    skip = skip_ref[0:1, :]
    for start in range(0, ROWS, LANES):
        rows = slice(start, start + LANES)
        turned = long_ref[:, start // LANES].reshape(LANES, LANES).T
        out_ref[rows, :] = gate_ref[rows, :] * (turned + skip * product_ref[rows, :])


def columns_of(chunk, slots):
    def column(i, z_ref):
        plane = z_ref[0]
        if slots == (1,):
            plane = 1 - plane
        elif len(slots) == 2:
            plane = jnp.where(i // 2 == 0, plane, 1 - plane)
        return plane * 2 + i % 2 + chunk * 4

    return column


def from_streams(kernel, streams, blocks, extra, out_shape, weight, z, projected, halo, short_filter, after):
    return pl.pallas_call(
        kernel,
        in_specs=[
            pl.BlockSpec(memory_space=pltpu.SMEM),
            pl.BlockSpec(memory_space=pl.ANY),
            pl.BlockSpec(memory_space=pltpu.HBM),
            pl.BlockSpec(memory_space=pltpu.HBM),
        ]
        + [pl.BlockSpec(memory_space=pl.ANY)] * len(after),
        out_specs=[pl.BlockSpec(memory_space=pl.ANY)] * len(out_shape),
        out_shape=out_shape,
        scratch_shapes=[
            pltpu.VMEM((blocks, streams, ROWS + 8, LANES), f32),
            pltpu.VMEM(halo.shape, f32),
            pltpu.VMEM(short_filter.shape, f32),
            pltpu.SemaphoreType.DMA((blocks + 1, 2)),
            pltpu.SemaphoreType.DMA((blocks, 2)),
        ]
        + extra,
        compiler_params=pltpu.CompilerParams(vmem_limit_bytes=VMEM_BYTES),
        cost_estimate=pl.CostEstimate(
            flops=weight * 1_000_000, bytes_accessed=1_000_000, transcendentals=0
        ),
        name="streams",
    )(z, halo, short_filter, projected, *after)


def features_of(z, chunk, slots, projected, halo, short_filter, after=(), weight=1):
    count = len(slots)
    blocks = 2 * count

    def columns_of_z(plane):
        planes = [plane if slot == 0 else 1 - plane for slot in slots for _ in range(2)]
        return [(chunk * 4 + planes[i] * 2 + i % 2) * LANES for i in range(blocks)]

    out_shape = [
        jax.ShapeDtypeStruct((PEERS, count * QUARTERS, PIECE, LANES), f32),
        jax.ShapeDtypeStruct((ROWS, blocks * LANES), f32),
    ]
    kernel = functools.partial(feature_kernel, columns_of_z)
    extra = [
        pltpu.VMEM((blocks, LANES // PIECE, QUARTERS, PIECE, LANES), f32),
        pltpu.VMEM((blocks, ROWS, LANES), f32),
    ]
    return from_streams(
        kernel, 2, blocks, extra, out_shape, weight, z, projected, halo, short_filter, after
    )


def gates_of(z, projected, halo, short_filter, after):
    out_shape = [jax.ShapeDtypeStruct((ROWS, 8 * LANES), f32)]
    return from_streams(
        gate_kernel, 1, 8, [pltpu.VMEM((8, ROWS, LANES), f32)], out_shape, SLOW, z, projected, halo, short_filter, after
    )[0]


def finish_own(z, b_out, gate, product_b, skip):
    column = columns_of(1, (0,))
    return pl.pallas_call(
        final_kernel,
        grid_spec=pltpu.PrefetchScalarGridSpec(
            num_scalar_prefetch=1,
            grid=(2,),
            in_specs=[
                pl.BlockSpec((LANES // PIECE, QUARTERS, PIECE, LANES), lambda i, z: (i, 0, 0, 0)),
                pl.BlockSpec((ROWS, LANES), lambda i, z: (0, column(i, z))),
                pl.BlockSpec((ROWS, LANES), lambda i, z: (0, i)),
                pl.BlockSpec((1, LANES), lambda i, z: (0, column(i, z))),
            ],
            out_specs=pl.BlockSpec((ROWS, LANES), lambda i, z: (0, column(i, z))),
        ),
        out_shape=jax.ShapeDtypeStruct((ROWS, 8 * LANES), f32),
        compiler_params=pltpu.CompilerParams(vmem_limit_bytes=VMEM_BYTES),
        cost_estimate=pl.CostEstimate(
            flops=SLOW * 1_000_000, bytes_accessed=1_000_000, transcendentals=0
        ),
        name="finish",
    )(z, b_out, gate, product_b, skip)


def finish_rest_kernel(
    z_ref,
    a_ref,
    b_ref,
    gate_ref,
    own_ref,
    other_ref,
    b_product_ref,
    skip_ref,
    whole_ref,
    out_ref,
    long_vmem,
    gate_vmem,
    product_vmem,
    out_vmem,
    in_sems,
    out_sems,
):
    z = z_ref[0]
    places = []
    arrivals = []
    for i in range(3):
        plane = z if i == 0 else 1 - z
        column = pl.multiple_of(((0 if i < 2 else 4) + plane * 2) * LANES, 2 * LANES)
        lanes = pl.ds(column, 2 * LANES)
        places.append(lanes)
        product = (own_ref, other_ref, b_product_ref)[i]
        flat = pl.ds((2 if i == 2 else 0) * LANES, 2 * LANES)
        pairs = [
            (a_ref.at[:, pl.ds(QUARTERS * i, QUARTERS)] if i < 2 else b_ref, long_vmem.at[i]),
            (gate_ref.at[:, lanes], gate_vmem.at[i]),
            (product.at[:, flat], product_vmem.at[i]),
        ]
        arrivals.append(copies_of(pairs, in_sems.at[i]))
    leaving = []
    for i in range(3):
        wait_all(arrivals[i])
        skip = skip_ref[0:1, places[i]]
        for quarter in range(QUARTERS):
            rows = slice(quarter * LANES, (quarter + 1) * LANES)
            turned = long_vmem[i, :, quarter].reshape(2 * LANES, LANES).T
            out_vmem[i, rows, :] = gate_vmem[i, rows, :] * (
                turned + skip * product_vmem[i, rows, :]
            )
        leaving = leaving + copies_of(
            [(out_vmem.at[i], out_ref.at[:, places[i]])], out_sems.at[i]
        )
    wait_all(leaving)


def finish_rest(z, a_out, b_back, gate, product_a, product_ao, product_b, skip, whole):
    operands = [z, a_out, b_back, gate, product_a, product_ao, product_b, skip, whole]
    anywhere = pl.BlockSpec(memory_space=pl.ANY)
    flat = pltpu.VMEM((3, ROWS, 2 * LANES), f32)
    return pl.pallas_call(
        finish_rest_kernel,
        in_specs=[pl.BlockSpec(memory_space=pltpu.SMEM)]
        + [anywhere] * 6
        + [pl.BlockSpec(memory_space=pltpu.VMEM), anywhere],
        out_specs=anywhere,
        out_shape=jax.ShapeDtypeStruct((ROWS, 8 * LANES), f32),
        scratch_shapes=[
            pltpu.VMEM((3, PEERS, QUARTERS, PIECE, LANES), f32),
            flat,
            flat,
            flat,
            pltpu.SemaphoreType.DMA((3, 3)),
            pltpu.SemaphoreType.DMA((3, 1)),
        ],
        input_output_aliases={len(operands) - 1: 0},
        compiler_params=pltpu.CompilerParams(vmem_limit_bytes=CONV_BYTES),
        cost_estimate=pl.CostEstimate(
            flops=1_000_000, bytes_accessed=1_000_000, transcendentals=0
        ),
        name="finish",
    )(*operands)


def convolve(z, layout, sources, tables, joined, after=()):
    if joined:
        out_shape = [jax.ShapeDtypeStruct((2 * HALF, LANES), f32)]
    else:
        out_shape = [
            jax.ShapeDtypeStruct((HALF, LANES), f32),
            jax.ShapeDtypeStruct((HALF, LANES), f32),
            jax.ShapeDtypeStruct((ORDER, 2 * LANES), f32),
        ]
    operands = list(sources) + [
        in_hbm(tables[name]) for name in ("first", "last", "onward", "back", "bend")
    ]
    anywhere = pl.BlockSpec(memory_space=pl.ANY)
    shapes = [(x.shape, x.dtype) for x in operands + out_shape]
    return pl.pallas_call(
        functools.partial(conv_kernel, layout, len(sources), len(out_shape), len(after)),
        in_specs=[pl.BlockSpec(memory_space=pltpu.SMEM)]
        + [anywhere] * (len(operands) + len(after)),
        out_specs=[anywhere] * len(out_shape),
        out_shape=out_shape,
        scratch_shapes=[pltpu.VMEM(shape, dtype) for shape, dtype in shapes]
        + [
            pltpu.SemaphoreType.DMA((len(operands), CUTS)),
            pltpu.SemaphoreType.DMA((len(out_shape), CUTS)),
        ],
        compiler_params=pltpu.CompilerParams(vmem_limit_bytes=CONV_BYTES),
        cost_estimate=pl.CostEstimate(
            flops=10_000_000, bytes_accessed=1_000_000, transcendentals=0
        ),
        name="convolve",
    )(z, *operands, *after)


def in_hbm(x):
    return pltpu.with_memory_space_constraint(x, pltpu.HBM)


def swap_planes(x):
    return lax.ppermute(x, "zh", [(0, 1), (1, 0)])


def across(x):
    return lax.all_to_all(x, PLANE, split_axis=0, concat_axis=0, tiled=True)


def relay(pairs, held_refs, in_sems, out_sems):
    arrivals, targets = [], []
    for at, ((source, target), held) in enumerate(zip(pairs, held_refs)):
        arrivals.append(copies_of(pieces_of(source, held, CUTS), in_sems.at[at]))
        targets.append(pieces_of(held, target, CUTS))
    leaving = []
    for cut in range(CUTS):
        for at in range(len(pairs)):
            arrivals[at][cut].wait()
            source, target = targets[at][cut]
            copy = pltpu.make_async_copy(source, target, out_sems.at[at, cut])
            copy.start()
            leaving.append(copy)
    return leaving


def join_taps_kernel(
    place_ref,
    own_ref,
    from_ref,
    here_ref,
    there_ref,
    after_ref,
    out_ref,
    own_held,
    from_held,
    in_sems,
    out_sems,
    taps_held,
    small_held,
    small_sems,
):
    pairs = [
        (own_ref, out_ref.at[:, pl.ds(0, QUARTERS)]),
        (from_ref, out_ref.at[:, pl.ds(QUARTERS, QUARTERS)]),
    ]
    small = [(here_ref, small_held.at[0]), (there_ref, small_held.at[1])]
    wait_all(copies_of(small, small_sems))
    leaving = relay(pairs, (own_held, from_held), in_sems, out_sems)
    z, group = place_ref[0], place_ref[1]
    for zq in range(8):
        row = (jnp.bitwise_xor(zq % 4, group) * 4) + group
        here = small_held[0, pl.ds(row, 1), :]
        there = small_held[1, pl.ds(row, 1), :]
        taps = jnp.where(z == zq // 4, here, there)
        taps_held[:, 0, zq : zq + 1, :] = jnp.broadcast_to(taps[None], (PEERS, 1, LANES))
    into = out_ref.at[:, pl.ds(2 * QUARTERS, 1)]
    wait_all(leaving + copies_of([(taps_held, into)], small_sems))


def join_kernel(own_ref, from_ref, after_ref, out_ref, own_held, from_held, in_sems, out_sems):
    pairs = [
        (own_ref, out_ref.at[:, pl.ds(0, QUARTERS)]),
        (from_ref, out_ref.at[:, pl.ds(QUARTERS, QUARTERS)]),
    ]
    wait_all(relay(pairs, (own_held, from_held), in_sems, out_sems))


def cut_kernel(both_ref, after_ref, out_ref, held, in_sems, out_sems):
    pairs = [(both_ref.at[:, pl.ds(QUARTERS, QUARTERS)], out_ref)]
    wait_all(relay(pairs, (held,), in_sems, out_sems))


def token_kernel(after_ref, out_ref):
    pass


def rearrange(kernel, operands, groups, pieces, place=None, cost=1_000):
    anywhere = pl.BlockSpec(memory_space=pl.ANY)
    scratch = [pltpu.VMEM((PEERS, QUARTERS, PIECE, LANES), f32)] * pieces
    scratch = scratch + [pltpu.SemaphoreType.DMA((pieces, CUTS))] * 2
    in_specs = [anywhere] * len(operands)
    if place is not None:
        scratch.append(pltpu.VMEM((PEERS, 1, PIECE, LANES), f32))
        scratch.append(pltpu.VMEM((2, 16, LANES), f32))
        scratch.append(pltpu.SemaphoreType.DMA((2,)))
        in_specs = [pl.BlockSpec(memory_space=pltpu.SMEM)] + in_specs
        operands = (place, *operands)
    return pl.pallas_call(
        kernel,
        in_specs=in_specs,
        out_specs=anywhere,
        out_shape=jax.ShapeDtypeStruct((PEERS, groups, PIECE, LANES), f32),
        scratch_shapes=scratch,
        compiler_params=pltpu.CompilerParams(vmem_limit_bytes=VMEM_BYTES),
        cost_estimate=pl.CostEstimate(flops=cost, bytes_accessed=1_000, transcendentals=0),
        name="rearrange",
    )(*operands)


def token(after):
    anywhere = pl.BlockSpec(memory_space=pl.ANY)
    return pl.pallas_call(
        token_kernel,
        in_specs=[anywhere],
        out_specs=anywhere,
        out_shape=jax.ShapeDtypeStruct((8, LANES), f32),
        cost_estimate=pl.CostEstimate(
            flops=SLOW * 1_000_000, bytes_accessed=1_000, transcendentals=0
        ),
        name="token",
    )(after)


def later_kernel(*refs):
    for at in range(4):
        refs[-1][at * 4 : (at + 1) * 4] = refs[at][...]


def later_rows(parts, after):
    inside = pl.BlockSpec(memory_space=pltpu.VMEM)
    return pl.pallas_call(
        later_kernel,
        in_specs=[inside] * 4 + [pl.BlockSpec(memory_space=pl.ANY)],
        out_specs=inside,
        out_shape=jax.ShapeDtypeStruct((16, LANES), f32),
        cost_estimate=pl.CostEstimate(flops=1_000, bytes_accessed=1_000, transcendentals=0),
        name="later",
    )(*parts, after)


def body(projected, short_filter, long_filter, skip_gain):
    tables = {name: jnp.asarray(table) for name, table in make_tables().items()}
    z = lax.axis_index("zh").astype(jnp.int32).reshape(1)
    skip = skip_gain.reshape(1, -1)
    devices = lax.axis_size(SEQ)
    halo = lax.ppermute(
        projected[:, ROWS - 8 :, :], SEQ, [(i, i + 1) for i in range(devices - 1)]
    )
    projected, short_filter = in_hbm(projected), in_hbm(short_filter)
    feature = functools.partial(
        features_of, projected=projected, halo=halo, short_filter=short_filter
    )
    a_other, product_ao = feature(z, 0, (1,))
    a_from = swap_planes(a_other)
    b_both, product_b = feature(z, 1, (0, 1), after=(product_ao,))
    b_here = across(b_both)
    a_own, product_a = feature(z, 0, (0,), after=(product_b,), weight=SLOW)

    steps = [
        lax.ppermute(long_filter, "zl", [(i, i ^ d) for i in range(4)]) for d in range(1, 4)
    ]
    taps_here = later_rows((long_filter, *steps), a_own)
    taps_there = swap_planes(taps_here)
    group = lax.axis_index("zl").astype(jnp.int32).reshape(1)
    place = jnp.concatenate([z, group])

    b_sent = rearrange(cut_kernel, (in_hbm(b_here), a_from), QUARTERS, 1)
    b_from = swap_planes(b_sent)
    a_sent = rearrange(
        join_taps_kernel,
        (in_hbm(a_own), a_from, taps_here, taps_there, in_hbm(b_sent)),
        2 * QUARTERS + 1,
        2,
        place=place,
        cost=10_000_000_000,
    )
    a_here = across(a_sent)
    gate = gates_of(z, projected, halo, short_filter, (a_from, b_here))
    wide = 2 * BLOCK + 8
    conv_a_own, conv_a_other, spectrum = convolve(
        z,
        (0, wide, BLOCK, wide, 2 * BLOCK),
        (in_hbm(a_here.reshape(-1, LANES)),),
        tables,
        False,
        (gate,),
    )

    a_back = swap_planes(conv_a_other.reshape(PEERS, QUARTERS, PIECE, LANES))
    (conv_b,) = convolve(
        z,
        (0, 2 * BLOCK, 0, BLOCK, None),
        (in_hbm(b_here.reshape(2 * HALF, LANES)), b_from.reshape(HALF, LANES), spectrum),
        tables,
        True,
    )
    b_out = across(conv_b.reshape(PEERS, 2 * QUARTERS, PIECE, LANES))

    a_kept = in_hbm(conv_a_own.reshape(PEERS, QUARTERS, PIECE, LANES))
    b_sent = rearrange(cut_kernel, (in_hbm(b_out), in_hbm(token(a_back))), QUARTERS, 1)
    b_back = swap_planes(b_sent)
    a_sent = rearrange(
        join_kernel, (a_kept, a_back, in_hbm(b_sent)), 2 * QUARTERS, 2, cost=10_000_000_000
    )
    a_out = across(a_sent)
    mixed = finish_own(z, b_out, in_hbm(gate), in_hbm(product_b), skip)
    return finish_rest(
        z,
        a_out,
        b_back,
        in_hbm(gate),
        in_hbm(product_a),
        in_hbm(product_ao),
        in_hbm(product_b),
        skip,
        mixed,
    )


def solution(mesh):
    fine = Mesh(mesh.devices.reshape(4, 2, 4, 2, 4), ("x", "zh", "y", "core", "zl"))
    placed = (P(None, SEQ, "zl"), P(None, None, "zl"), P(None, SEQ + ("zl",)), P("zl"))
    return jax.shard_map(
        body, mesh=fine, in_specs=placed, out_specs=P(SEQ, "zl"), check_vma=False
    )
```

```python
import functools

import jax
import jax.numpy as jnp
import ml_dtypes
import numpy as np
from jax import lax
from jax.experimental import pallas as pl
from jax.experimental.pallas import tpu as pltpu
from jax.sharding import Mesh
from jax.sharding import PartitionSpec as P

f32 = jnp.float32
bf16 = jnp.bfloat16

ROWS = 512
TAPS = 7
LANES = 128
PEERS = 32
PIECE = 8
QUARTERS = ROWS // LANES
BLOCK = QUARTERS * PIECE
HALF = PEERS * BLOCK
LENGTH = 32768
VMEM_BYTES = 16 << 20
CONV_BYTES = 40 << 20
WHOLE_BYTES = 40 << 20
SLOW = 200_000
ORDER = 256

SEQ = ("x", "zh", "y", "core")
PLANE = ("x", "y", "core")


def split_np(table):
    high = table.astype(np.float32).astype(ml_dtypes.bfloat16)
    low = (table - high.astype(np.float64)).astype(ml_dtypes.bfloat16)
    return high, low


def position_blocks():
    n1 = np.zeros((2, 4, PEERS), np.int64)
    for z in range(2):
        for q in range(4):
            for p in range(PEERS):
                x, rest = divmod(p, 8)
                n1[z, q, p] = 4 * (x * 16 + z * 8 + rest) + q
    return n1.reshape(-1)


def make_tables():
    n1 = position_blocks()
    k1 = np.arange(ORDER)
    m = np.arange(LANES)
    turn = 2.0 * np.pi
    first = turn * (((4 * k1[:, None] + 1) * n1[None, :]) % (4 * ORDER)) / (4 * ORDER)
    first = np.concatenate([np.cos(first), -np.sin(first)], axis=0)
    bend = turn * ((4 * k1[:, None] + 1) * m[None, :]) / (4 * LENGTH)
    second = turn * ((m[:, None] * m[None, :]) % LANES) / LANES
    cosine, sine = np.cos(second), np.sin(second)
    onward = np.block([[cosine, -sine], [sine, cosine]])
    back = np.block([[cosine, sine], [-sine, cosine]])
    last = first.T
    first_high, first_low = split_np(first)
    onward_high, onward_low = split_np(onward)
    back_high, back_low = split_np(back)
    last_high, last_low = split_np(last)
    return dict(
        first=np.concatenate([first_high, first_low], axis=1),
        last=np.concatenate([last_high, last_low], axis=1),
        onward=np.concatenate([onward_high, onward_low], axis=0),
        back=np.concatenate([back_high, back_low], axis=0),
        bend=np.stack([np.cos(bend), -np.sin(bend)]).astype(np.float32),
    )


def halves(x):
    high = x.astype(bf16)
    low = (x - high.astype(f32)).astype(bf16)
    return high, low


def thrice(table, axis):
    half = table.shape[axis] // 2
    high = lax.slice_in_dim(table, 0, half, axis=axis)
    return jnp.concatenate([high, table], axis=axis)


def dot(a, b):
    return jnp.dot(a, b, preferred_element_type=f32)


def to_spectrum(columns, first, onward, bend):
    high, low = halves(columns)
    section = dot(first, jnp.concatenate([high, low, high], axis=0))
    bend_re, bend_im = bend[0], bend[1]
    rows = []
    for at in range(columns.shape[1] // LANES):
        re = section[:ORDER, at * LANES : (at + 1) * LANES]
        im = section[ORDER:, at * LANES : (at + 1) * LANES]
        rows.append(
            jnp.concatenate([re * bend_re - im * bend_im, re * bend_im + im * bend_re], axis=1)
        )
    bent = jnp.concatenate(rows, axis=0)
    high, low = halves(bent)
    return dot(jnp.concatenate([high, low, high], axis=1), onward)


def from_spectrum(spectrum, last, back, bend):
    high, low = halves(spectrum)
    section = dot(jnp.concatenate([high, low, high], axis=1), back)
    bend_re, bend_im = bend[0], bend[1]
    columns = []
    for at in range(spectrum.shape[0] // ORDER):
        re = section[at * ORDER : (at + 1) * ORDER, :LANES]
        im = section[at * ORDER : (at + 1) * ORDER, LANES:]
        columns.append(
            jnp.concatenate([re * bend_re + im * bend_im, im * bend_re - re * bend_im], axis=0)
        )
    bent = jnp.concatenate(columns, axis=1)
    high, low = halves(bent)
    return dot(last, jnp.concatenate([high, low, high], axis=0))


def pieces_of(source_ref, target_ref, count):
    count = min(count, source_ref.shape[0])
    rows = source_ref.shape[0] // count
    cuts = [pl.ds(at * rows, rows) for at in range(count)]
    return [(source_ref.at[cut], target_ref.at[cut]) for cut in cuts]


def copies_of(pairs, sems):
    copies = [
        pltpu.make_async_copy(source, target, sems.at[at])
        for at, (source, target) in enumerate(pairs)
    ]
    for copy in copies:
        copy.start()
    return copies


def wait_all(copies):
    for copy in copies:
        copy.wait()


CUTS = 1


BATCH = 2
LAG = 1


def pieces_taps(ref, at, stride):
    return jnp.concatenate([ref[pl.ds(at + zq, PEERS, stride=stride), :] for zq in range(8)], axis=0)


def conv_kernel(layout, sources, outputs, after, z_ref, *refs):
    own_at, own_stride, other_at, other_stride, taps_at = layout
    inputs = sources + 5
    given, results = refs[:inputs], refs[inputs + after : inputs + after + outputs]
    held = refs[inputs + after + outputs : -2]
    in_sems, out_sems = refs[-2:]
    order = list(range(sources)) + [sources + at for at in (0, 4, 2, 3, 1)]
    arrivals = {}
    for k in order:
        arrivals[k] = copies_of(pieces_of(given[k], held[k], CUTS), in_sems.at[k])
    own_ref, other_ref, spectrum_ref = (held[:sources] * 3)[:3]
    first_ref, last_ref, onward_ref, back_ref, bend_ref = held[sources:inputs]
    out_refs = held[inputs:]
    low_plane = z_ref[0] == 0

    for k in range(sources):
        wait_all(arrivals[k])
    extra = [pieces_taps(spectrum_ref, taps_at, own_stride)] if taps_at is not None else []
    wait_all(arrivals[sources] + arrivals[sources + 4] + arrivals[sources + 2])
    bend = bend_ref[...]
    bend_re, bend_im = bend[0], bend[1]
    leaving = []
    if taps_at is not None:
        taps = to_spectrum(extra[0], thrice(first_ref[...], 1), thrice(onward_ref[...], 0), bend) * (1.0 / LENGTH)
        out_refs[2][...] = taps
        leaving = copies_of(pieces_of(out_refs[2], results[2], 1), out_sems.at[2])
    else:
        taps = spectrum_ref[...]
    taps_re = taps[:, :LANES]
    taps_im = taps[:, LANES:]

    def gather(at):
        own, other = [], []
        for q in range(4):
            row = q * PIECE + at
            own.append(own_ref[pl.ds(own_at + row, PEERS, stride=own_stride), :])
            other.append(other_ref[pl.ds(other_at + row, PEERS, stride=other_stride), :])
        own = jnp.concatenate(own, axis=0)
        other = jnp.concatenate(other, axis=0)
        return jnp.concatenate(
            [jnp.where(low_plane, own, other), jnp.where(low_plane, other, own)], axis=0
        )

    def store(at, column):
        upper, lower = column[: ORDER // 2], column[ORDER // 2 :]
        own = jnp.where(low_plane, upper, lower)
        other = jnp.where(low_plane, lower, upper)
        for q in range(4):
            row = q * PIECE + at
            rows_own = own[q * PEERS : (q + 1) * PEERS]
            rows_other = other[q * PEERS : (q + 1) * PEERS]
            out_refs[0][pl.ds(row, PEERS, stride=BLOCK), :] = rows_own
            out_refs[1][pl.ds(row, PEERS, stride=BLOCK), :] = rows_other

    def load(channels):
        high, low = halves(jnp.concatenate([gather(at) for at in channels], axis=1))
        return jnp.concatenate([high, low, high], axis=0)

    def to_blocks(x):
        return dot(thrice(first_ref[...], 1), x)

    def bend_onward(section):
        rows = []
        for at in range(section.shape[1] // LANES):
            re = section[:ORDER, at * LANES : (at + 1) * LANES]
            im = section[ORDER:, at * LANES : (at + 1) * LANES]
            rows.append(
                jnp.concatenate([re * bend_re - im * bend_im, re * bend_im + im * bend_re], axis=1)
            )
        high, low = halves(jnp.concatenate(rows, axis=0))
        return jnp.concatenate([high, low, high], axis=1)

    def to_frequencies(x):
        return dot(x, thrice(onward_ref[...], 0))

    def weigh(spectrum):
        rows = []
        for at in range(spectrum.shape[0] // ORDER):
            re = spectrum[at * ORDER : (at + 1) * ORDER, :LANES]
            im = spectrum[at * ORDER : (at + 1) * ORDER, LANES:]
            rows.append(
                jnp.concatenate([re * taps_re - im * taps_im, re * taps_im + im * taps_re], axis=1)
            )
        high, low = halves(jnp.concatenate(rows, axis=0))
        return jnp.concatenate([high, low, high], axis=1)

    def from_frequencies(x):
        return dot(x, thrice(back_ref[...], 0))

    def bend_back(section):
        columns = []
        for at in range(section.shape[0] // ORDER):
            re = section[at * ORDER : (at + 1) * ORDER, :LANES]
            im = section[at * ORDER : (at + 1) * ORDER, LANES:]
            columns.append(
                jnp.concatenate([re * bend_re + im * bend_im, im * bend_re - re * bend_im], axis=0)
            )
        high, low = halves(jnp.concatenate(columns, axis=1))
        return jnp.concatenate([high, low, high], axis=0)

    def from_blocks(x):
        return dot(thrice(last_ref[...], 1), x)

    stages = (
        load, to_blocks, bend_onward, to_frequencies, weigh, from_frequencies, bend_back, from_blocks
    )
    batches = [tuple(range(at, at + BATCH)) for at in range(0, PIECE, BATCH)]
    state = list(batches)
    for tick in range(len(stages) + 1 + LAG * (len(batches) - 1)):
        if tick == 5:
            wait_all(arrivals[sources + 3] + arrivals[sources + 1])
        for batch, channels in enumerate(batches):
            stage = tick - LAG * batch
            if 0 <= stage < len(stages):
                state[batch] = stages[stage](state[batch])
            elif stage == len(stages):
                for at, channel in enumerate(channels):
                    store(channel, state[batch][:, at * LANES : (at + 1) * LANES])
    for k in (1, 0):
        leaving = leaving + copies_of(pieces_of(out_refs[k], results[k], CUTS), out_sems.at[k])
    wait_all(leaving)


def short_sum(short, long_ref, at, step):
    total = short[0:1] * long_ref[at + 2 : at + 2 + step, :]
    for i in range(1, TAPS):
        total = total + short[i : i + 1] * long_ref[at + 2 + i : at + 2 + i + step, :]
    return total


def fetch(proj_ref, halo_ref, short_ref, buffer_ref, halo_held, taps_held, sems, streams, columns):
    edges = copies_of([(halo_ref, halo_held), (short_ref, taps_held)], sems.at[len(columns)])
    first, count = streams
    blocks = []
    for i, column in enumerate(columns):
        lanes = pl.ds(pl.multiple_of(column, LANES), LANES)
        copy = pltpu.make_async_copy(
            proj_ref.at[pl.ds(first, count), :, lanes],
            buffer_ref.at[i, :, pl.ds(8, ROWS)],
            sems.at[i, 0],
        )
        copy.start()
        blocks.append(copy)
    wait_all(edges)
    for i, column in enumerate(columns):
        lanes = pl.ds(pl.multiple_of(column, LANES), LANES)
        buffer_ref[i, :, 0:8, :] = halo_held[first : first + count, :, lanes]
    return blocks


def feature_kernel(columns_of_z, z_ref, halo_ref, short_ref, proj_ref, *rest):
    sent_ref, product_ref = rest[-9:-7]
    buffer_ref, halo_held, taps_held, sems, out_sems, turned_ref, flat_ref = rest[-7:]
    step = 64
    columns = columns_of_z(z_ref[0])
    blocks = fetch(
        proj_ref, halo_ref, short_ref, buffer_ref, halo_held, taps_held, sems, (1, 2), columns
    )
    peers = LANES // PIECE
    leaving = []
    for i, copy in enumerate(blocks):
        copy.wait()
        lanes = pl.ds(pl.multiple_of(columns[i], LANES), LANES)
        key_taps, value_taps = taps_held[1, :, lanes], taps_held[2, :, lanes]
        for quarter in range(QUARTERS):
            parts = []
            for at in range(quarter * LANES, (quarter + 1) * LANES, step):
                product = short_sum(key_taps, buffer_ref.at[i, 0], at, step) * short_sum(
                    value_taps, buffer_ref.at[i, 1], at, step
                )
                flat_ref[i, at : at + step, :] = product
                parts.append(product)
            turned = jnp.concatenate(parts, axis=0).T
            turned_ref[i, :, quarter] = turned.reshape(peers, PIECE, LANES)
        into = sent_ref.at[
            pl.ds(i % 2 * peers, peers), pl.ds(i // 2 * QUARTERS, QUARTERS)
        ]
        pairs = [(turned_ref.at[i], into)]
        pairs.append((flat_ref.at[i], product_ref.at[:, pl.ds(i * LANES, LANES)]))
        leaving = leaving + copies_of(pairs, out_sems.at[i])
    wait_all(leaving)


def gate_kernel(chunk, z_ref, halo_ref, short_ref, proj_ref, *rest):
    gate_ref, buffer_ref, halo_held, taps_held, sems, out_sems, flat_ref = rest[-7:]
    step = 64
    columns = [(chunk * 4 + i) * LANES for i in range(4)]
    blocks = fetch(
        proj_ref, halo_ref, short_ref, buffer_ref, halo_held, taps_held, sems, (0, 1), columns
    )
    leaving = []
    for i, copy in enumerate(blocks):
        copy.wait()
        taps = taps_held[0, :, columns[i] : columns[i] + LANES]
        for at in range(0, ROWS, step):
            flat_ref[i, at : at + step, :] = short_sum(taps, buffer_ref.at[i, 0], at, step)
        pairs = [(flat_ref.at[i], gate_ref.at[:, pl.ds(i * LANES, LANES)])]
        leaving = leaving + copies_of(pairs, out_sems.at[i])
    wait_all(leaving)


def from_streams(kernel, streams, blocks, extra, out_shape, weight, z, projected, halo, short_filter, after):
    return pl.pallas_call(
        kernel,
        in_specs=[
            pl.BlockSpec(memory_space=pltpu.SMEM),
            pl.BlockSpec(memory_space=pl.ANY),
            pl.BlockSpec(memory_space=pltpu.HBM),
            pl.BlockSpec(memory_space=pltpu.HBM),
        ]
        + [pl.BlockSpec(memory_space=pl.ANY)] * len(after),
        out_specs=[pl.BlockSpec(memory_space=pl.ANY)] * len(out_shape),
        out_shape=out_shape,
        scratch_shapes=[
            pltpu.VMEM((blocks, streams, ROWS + 8, LANES), f32),
            pltpu.VMEM(halo.shape, f32),
            pltpu.VMEM(short_filter.shape, f32),
            pltpu.SemaphoreType.DMA((blocks + 1, 2)),
            pltpu.SemaphoreType.DMA((blocks, 2)),
        ]
        + extra,
        compiler_params=pltpu.CompilerParams(vmem_limit_bytes=WHOLE_BYTES),
        cost_estimate=pl.CostEstimate(
            flops=weight * 1_000_000, bytes_accessed=1_000_000, transcendentals=0
        ),
        name="streams",
    )(z, halo, short_filter, projected, *after)


def features_of(z, parts, projected, halo, short_filter, after=(), weight=1):
    blocks = 2 * len(parts)

    def columns_of_z(plane):
        firsts = [chunk * 4 + (1 - plane if slot else plane) * 2 for chunk, slot in parts]
        return [(firsts[i // 2] + i % 2) * LANES for i in range(blocks)]

    out_shape = [
        jax.ShapeDtypeStruct((PEERS, len(parts) * QUARTERS, PIECE, LANES), f32),
        jax.ShapeDtypeStruct((ROWS, blocks * LANES), f32),
    ]
    kernel = functools.partial(feature_kernel, columns_of_z)
    extra = [
        pltpu.VMEM((blocks, LANES // PIECE, QUARTERS, PIECE, LANES), f32),
        pltpu.VMEM((blocks, ROWS, LANES), f32),
    ]
    return from_streams(
        kernel, 2, blocks, extra, out_shape, weight, z, projected, halo, short_filter, after
    )


def gates_of(z, chunk, projected, halo, short_filter, after):
    out_shape = [jax.ShapeDtypeStruct((ROWS, 4 * LANES), f32)]
    kernel = functools.partial(gate_kernel, chunk)
    extra = [pltpu.VMEM((4, ROWS, LANES), f32)]
    return from_streams(
        kernel, 1, 4, extra, out_shape, SLOW, z, projected, halo, short_filter, after
    )[0]


def finish_kernel(
    z_ref,
    out_part_ref,
    b_ref,
    gate_a_ref,
    gate_b_ref,
    own_ref,
    a_product_ref,
    b_product_ref,
    skip_ref,
    out_ref,
    long_vmem,
    gate_vmem,
    product_vmem,
    out_vmem,
    in_sems,
    out_sems,
):
    z = z_ref[0]
    wide = 2 * LANES
    places = []
    arrivals = []
    for i in range(4):
        plane = 1 - z if i % 2 else z
        column = pl.multiple_of((i // 2 * 4 + plane * 2) * LANES, wide)
        lanes = pl.ds(column, wide)
        places.append(lanes)
        half = pl.ds(pl.multiple_of(plane * wide, wide), wide)
        if i % 2:
            product = (a_product_ref, b_product_ref)[i // 2]
        else:
            product = own_ref.at[:, pl.ds(i // 2 * wide, wide)]
        long = out_part_ref.at[:, pl.ds(QUARTERS * i, QUARTERS)] if i < 3 else b_ref
        pairs = [
            (long, long_vmem.at[i]),
            ((gate_a_ref, gate_b_ref)[i // 2].at[:, half], gate_vmem.at[i]),
            (product, product_vmem.at[i]),
        ]
        arrivals.append(copies_of(pairs, in_sems.at[i]))
    leaving = []
    for i in range(4):
        wait_all(arrivals[i])
        skip = skip_ref[0:1, places[i]]
        for quarter in range(QUARTERS):
            rows = slice(quarter * LANES, (quarter + 1) * LANES)
            turned = long_vmem[i, :, quarter].reshape(wide, LANES).T
            out_vmem[i, rows, :] = gate_vmem[i, rows, :] * (
                turned + skip * product_vmem[i, rows, :]
            )
        leaving = leaving + copies_of(
            [(out_vmem.at[i], out_ref.at[:, places[i]])], out_sems.at[i]
        )
    wait_all(leaving)


def finish(z, out_part, b_back, gate_a, gate_b, product_own, product_a, product_b, skip):
    anywhere = pl.BlockSpec(memory_space=pl.ANY)
    flat = pltpu.VMEM((4, ROWS, 2 * LANES), f32)
    return pl.pallas_call(
        finish_kernel,
        in_specs=[pl.BlockSpec(memory_space=pltpu.SMEM)]
        + [anywhere] * 7
        + [pl.BlockSpec(memory_space=pltpu.VMEM)],
        out_specs=anywhere,
        out_shape=jax.ShapeDtypeStruct((ROWS, 8 * LANES), f32),
        scratch_shapes=[
            pltpu.VMEM((4, PEERS, QUARTERS, PIECE, LANES), f32),
            flat,
            flat,
            flat,
            pltpu.SemaphoreType.DMA((4, 3)),
            pltpu.SemaphoreType.DMA((4, 1)),
        ],
        compiler_params=pltpu.CompilerParams(vmem_limit_bytes=CONV_BYTES),
        cost_estimate=pl.CostEstimate(
            flops=1_000_000, bytes_accessed=1_000_000, transcendentals=0
        ),
        name="finish",
    )(z, out_part, b_back, gate_a, gate_b, product_own, product_a, product_b, skip)


def convolve(z, layout, sources, tables, after=()):
    out_shape = [jax.ShapeDtypeStruct((HALF, LANES), f32)] * 2
    if layout[-1] is not None:
        out_shape = out_shape + [jax.ShapeDtypeStruct((ORDER, 2 * LANES), f32)]
    operands = list(sources) + [
        in_hbm(tables[name]) for name in ("first", "last", "onward", "back", "bend")
    ]
    anywhere = pl.BlockSpec(memory_space=pl.ANY)
    shapes = [(x.shape, x.dtype) for x in operands + out_shape]
    return pl.pallas_call(
        functools.partial(conv_kernel, layout, len(sources), len(out_shape), len(after)),
        in_specs=[pl.BlockSpec(memory_space=pltpu.SMEM)]
        + [anywhere] * (len(operands) + len(after)),
        out_specs=[anywhere] * len(out_shape),
        out_shape=out_shape,
        scratch_shapes=[pltpu.VMEM(shape, dtype) for shape, dtype in shapes]
        + [
            pltpu.SemaphoreType.DMA((len(operands), CUTS)),
            pltpu.SemaphoreType.DMA((len(out_shape), CUTS)),
        ],
        compiler_params=pltpu.CompilerParams(vmem_limit_bytes=WHOLE_BYTES),
        cost_estimate=pl.CostEstimate(
            flops=10_000_000, bytes_accessed=1_000_000, transcendentals=0
        ),
        name="convolve",
    )(z, *operands, *after)


def in_hbm(x):
    return pltpu.with_memory_space_constraint(x, pltpu.HBM)


def swap_planes(x):
    return lax.ppermute(x, "zh", [(0, 1), (1, 0)])


def across(x):
    return lax.all_to_all(x, PLANE, split_axis=0, concat_axis=0, tiled=True)


def relay(pairs, held_refs, in_sems, out_sems):
    arrivals, targets = [], []
    for at, ((source, target), held) in enumerate(zip(pairs, held_refs)):
        arrivals.append(copies_of(pieces_of(source, held, CUTS), in_sems.at[at]))
        targets.append(pieces_of(held, target, CUTS))
    leaving = []
    for cut in range(CUTS):
        for at in range(len(pairs)):
            arrivals[at][cut].wait()
            source, target = targets[at][cut]
            copy = pltpu.make_async_copy(source, target, out_sems.at[at, cut])
            copy.start()
            leaving.append(copy)
    return leaving


def join_taps_kernel(
    place_ref,
    own_ref,
    from_ref,
    here_ref,
    there_ref,
    out_ref,
    own_held,
    from_held,
    in_sems,
    out_sems,
    taps_held,
    small_held,
    small_sems,
):
    pairs = [
        (own_ref, out_ref.at[:, pl.ds(0, 2 * QUARTERS)]),
        (from_ref, out_ref.at[:, pl.ds(2 * QUARTERS, QUARTERS)]),
    ]
    small = [(here_ref, small_held.at[0]), (there_ref, small_held.at[1])]
    wait_all(copies_of(small, small_sems))
    leaving = relay(pairs, (own_held, from_held), in_sems, out_sems)
    z, group = place_ref[0], place_ref[1]
    for zq in range(8):
        row = (jnp.bitwise_xor(zq % 4, group) * 4) + group
        here = small_held[0, pl.ds(row, 1), :]
        there = small_held[1, pl.ds(row, 1), :]
        taps = jnp.where(z == zq // 4, here, there)
        taps_held[:, 0, zq : zq + 1, :] = jnp.broadcast_to(taps[None], (PEERS, 1, LANES))
    into = out_ref.at[:, pl.ds(3 * QUARTERS, 1)]
    wait_all(leaving + copies_of([(taps_held, into)], small_sems))


def join_kernel(a_ref, from_ref, b_ref, out_ref, a_held, from_held, b_held, in_sems, out_sems):
    pairs = [
        (ref, out_ref.at[:, pl.ds(QUARTERS * at, QUARTERS)])
        for at, ref in enumerate((a_ref, from_ref, b_ref))
    ]
    wait_all(relay(pairs, (a_held, from_held, b_held), in_sems, out_sems))


def rearrange(kernel, operands, groups, pieces, place=None, cost=10_000_000_000):
    anywhere = pl.BlockSpec(memory_space=pl.ANY)
    scratch = [pltpu.VMEM(x.shape, f32) for x in operands[:pieces]]
    scratch = scratch + [pltpu.SemaphoreType.DMA((pieces, CUTS))] * 2
    in_specs = [anywhere] * len(operands)
    if place is not None:
        scratch.append(pltpu.VMEM((PEERS, 1, PIECE, LANES), f32))
        scratch.append(pltpu.VMEM((2, 16, LANES), f32))
        scratch.append(pltpu.SemaphoreType.DMA((2,)))
        in_specs = [pl.BlockSpec(memory_space=pltpu.SMEM)] + in_specs
        operands = (place, *operands)
    return pl.pallas_call(
        kernel,
        in_specs=in_specs,
        out_specs=anywhere,
        out_shape=jax.ShapeDtypeStruct((PEERS, groups, PIECE, LANES), f32),
        scratch_shapes=scratch,
        compiler_params=pltpu.CompilerParams(vmem_limit_bytes=VMEM_BYTES),
        cost_estimate=pl.CostEstimate(flops=cost, bytes_accessed=1_000, transcendentals=0),
        name="rearrange",
    )(*operands)


def later_kernel(*refs):
    for at in range(4):
        refs[-1][at * 4 : (at + 1) * 4] = refs[at][...]


def later_rows(parts, after):
    inside = pl.BlockSpec(memory_space=pltpu.VMEM)
    return pl.pallas_call(
        later_kernel,
        in_specs=[inside] * 4 + [pl.BlockSpec(memory_space=pl.ANY)],
        out_specs=inside,
        out_shape=jax.ShapeDtypeStruct((16, LANES), f32),
        cost_estimate=pl.CostEstimate(flops=1_000, bytes_accessed=1_000, transcendentals=0),
        name="later",
    )(*parts, after)


def body(projected, short_filter, long_filter, skip_gain):
    tables = {name: jnp.asarray(table) for name, table in make_tables().items()}
    z = lax.axis_index("zh").astype(jnp.int32).reshape(1)
    skip = skip_gain.reshape(1, -1)
    devices = lax.axis_size(SEQ)
    halo = lax.ppermute(
        projected[:, ROWS - 8 :, :], SEQ, [(i, i + 1) for i in range(devices - 1)]
    )
    projected, short_filter = in_hbm(projected), in_hbm(short_filter)
    feature = functools.partial(
        features_of, projected=projected, halo=halo, short_filter=short_filter
    )
    a_other, product_a = feature(z, ((0, 1),))
    a_from = swap_planes(a_other)
    b_other, product_b = feature(z, ((1, 1),), after=(product_a,))
    b_there = across(b_other)
    own, product_own = feature(z, ((0, 0), (1, 0)), after=(product_b,), weight=SLOW)

    steps = [
        lax.ppermute(long_filter, "zl", [(i, i ^ d) for i in range(4)]) for d in range(1, 4)
    ]
    taps_here = later_rows((long_filter, *steps), own)
    taps_there = swap_planes(taps_here)
    group = lax.axis_index("zl").astype(jnp.int32).reshape(1)
    place = jnp.concatenate([z, group])

    b_from = swap_planes(b_there)
    sent = rearrange(
        join_taps_kernel,
        (in_hbm(own), a_from, taps_here, taps_there),
        3 * QUARTERS + 1,
        2,
        place=place,
    )
    here = across(sent).reshape(-1, LANES)
    gate_a = gates_of(z, 0, projected, halo, short_filter, (a_from, b_there))
    wide = 3 * BLOCK + 8
    conv_a_own, conv_a_other, spectrum = convolve(
        z, (0, wide, 2 * BLOCK, wide, 3 * BLOCK), (in_hbm(here),), tables, (gate_a,)
    )

    pieces = (PEERS, QUARTERS, PIECE, LANES)
    a_back = swap_planes(conv_a_other.reshape(pieces))
    conv_b_own, conv_b_other = convolve(
        z,
        (BLOCK, wide, 0, BLOCK, None),
        (in_hbm(here), b_from.reshape(HALF, LANES), spectrum),
        tables,
    )
    b_out = across(conv_b_other.reshape(pieces))

    b_back = swap_planes(b_out)
    gate_b = gates_of(z, 1, projected, halo, short_filter, (a_back, b_out))
    sent = rearrange(
        join_kernel,
        (in_hbm(conv_a_own.reshape(pieces)), a_back, in_hbm(conv_b_own.reshape(pieces))),
        3 * QUARTERS,
        3,
    )
    out_part = across(sent)
    return finish(
        z,
        out_part,
        b_back,
        in_hbm(gate_a),
        in_hbm(gate_b),
        in_hbm(product_own),
        in_hbm(product_a),
        in_hbm(product_b),
        skip,
    )


def solution(mesh):
    fine = Mesh(mesh.devices.reshape(4, 2, 4, 2, 4), ("x", "zh", "y", "core", "zl"))
    placed = (P(None, SEQ, "zl"), P(None, None, "zl"), P(None, SEQ + ("zl",)), P("zl"))
    return jax.shard_map(
        body, mesh=fine, in_specs=placed, out_specs=P(SEQ, "zl"), check_vma=False
    )
```

```python
import functools

import jax
import jax.numpy as jnp
import ml_dtypes
import numpy as np
from jax import lax
from jax.experimental import pallas as pl
from jax.experimental.pallas import tpu as pltpu
from jax.sharding import Mesh
from jax.sharding import PartitionSpec as P

f32 = jnp.float32
bf16 = jnp.bfloat16

ROWS = 512
TAPS = 7
LANES = 128
PEERS = 32
PIECE = 8
QUARTERS = ROWS // LANES
BLOCK = QUARTERS * PIECE
HALF = PEERS * BLOCK
LENGTH = 32768
VMEM_BYTES = 16 << 20
CONV_BYTES = 40 << 20
WHOLE_BYTES = 40 << 20
SLOW = 200_000
ORDER = 256

SEQ = ("x", "zh", "y", "core")
PLANE = ("x", "y", "core")


def split_np(table):
    high = table.astype(np.float32).astype(ml_dtypes.bfloat16)
    low = (table - high.astype(np.float64)).astype(ml_dtypes.bfloat16)
    return high, low


def position_blocks():
    n1 = np.zeros((2, 4, PEERS), np.int64)
    for z in range(2):
        for q in range(4):
            for p in range(PEERS):
                x, rest = divmod(p, 8)
                n1[z, q, p] = 4 * (x * 16 + z * 8 + rest) + q
    return n1.reshape(-1)


def make_tables():
    n1 = position_blocks()
    k1 = np.arange(ORDER)
    m = np.arange(LANES)
    turn = 2.0 * np.pi
    first = turn * (((4 * k1[:, None] + 1) * n1[None, :]) % (4 * ORDER)) / (4 * ORDER)
    first = np.concatenate([np.cos(first), -np.sin(first)], axis=0)
    bend = turn * ((4 * k1[:, None] + 1) * m[None, :]) / (4 * LENGTH)
    second = turn * ((m[:, None] * m[None, :]) % LANES) / LANES
    cosine, sine = np.cos(second), np.sin(second)
    onward = np.block([[cosine, -sine], [sine, cosine]])
    back = np.block([[cosine, sine], [-sine, cosine]])
    last = first.T
    first_high, first_low = split_np(first)
    onward_high, onward_low = split_np(onward)
    back_high, back_low = split_np(back)
    last_high, last_low = split_np(last)
    return dict(
        first=np.concatenate([first_high, first_low], axis=1),
        last=np.concatenate([last_high, last_low], axis=1),
        onward=np.concatenate([onward_high, onward_low], axis=0),
        back=np.concatenate([back_high, back_low], axis=0),
        bend=np.stack([np.cos(bend), -np.sin(bend)]).astype(np.float32),
    )


def halves(x):
    high = x.astype(bf16)
    low = (x - high.astype(f32)).astype(bf16)
    return high, low


def thrice(table, axis):
    half = table.shape[axis] // 2
    high = lax.slice_in_dim(table, 0, half, axis=axis)
    return jnp.concatenate([high, table], axis=axis)


def dot(a, b):
    return jnp.dot(a, b, preferred_element_type=f32)


def to_spectrum(columns, first, onward, bend):
    high, low = halves(columns)
    section = dot(first, jnp.concatenate([high, low, high], axis=0))
    bend_re, bend_im = bend[0], bend[1]
    rows = []
    for at in range(columns.shape[1] // LANES):
        re = section[:ORDER, at * LANES : (at + 1) * LANES]
        im = section[ORDER:, at * LANES : (at + 1) * LANES]
        rows.append(
            jnp.concatenate([re * bend_re - im * bend_im, re * bend_im + im * bend_re], axis=1)
        )
    bent = jnp.concatenate(rows, axis=0)
    high, low = halves(bent)
    return dot(jnp.concatenate([high, low, high], axis=1), onward)


def from_spectrum(spectrum, last, back, bend):
    high, low = halves(spectrum)
    section = dot(jnp.concatenate([high, low, high], axis=1), back)
    bend_re, bend_im = bend[0], bend[1]
    columns = []
    for at in range(spectrum.shape[0] // ORDER):
        re = section[at * ORDER : (at + 1) * ORDER, :LANES]
        im = section[at * ORDER : (at + 1) * ORDER, LANES:]
        columns.append(
            jnp.concatenate([re * bend_re + im * bend_im, im * bend_re - re * bend_im], axis=0)
        )
    bent = jnp.concatenate(columns, axis=1)
    high, low = halves(bent)
    return dot(last, jnp.concatenate([high, low, high], axis=0))


def pieces_of(source_ref, target_ref, count):
    count = min(count, source_ref.shape[0])
    rows = source_ref.shape[0] // count
    cuts = [pl.ds(at * rows, rows) for at in range(count)]
    return [(source_ref.at[cut], target_ref.at[cut]) for cut in cuts]


def copies_of(pairs, sems):
    copies = [
        pltpu.make_async_copy(source, target, sems.at[at])
        for at, (source, target) in enumerate(pairs)
    ]
    for copy in copies:
        copy.start()
    return copies


def wait_all(copies):
    for copy in copies:
        copy.wait()


CUTS = 1


BATCH = 2
LAG = 1


def pieces_taps(ref, at, stride):
    return jnp.concatenate([ref[pl.ds(at + zq, PEERS, stride=stride), :] for zq in range(8)], axis=0)


def conv_kernel(layout, sources, outputs, after, z_ref, *refs):
    own_at, own_stride, other_at, other_stride, taps_at = layout
    inputs = sources + 5
    given, results = refs[:inputs], refs[inputs + after : inputs + after + outputs]
    held = refs[inputs + after + outputs : -2]
    in_sems, out_sems = refs[-2:]
    order = list(range(sources)) + [sources + at for at in (0, 4, 2, 3, 1)]
    arrivals = {}
    for k in order:
        arrivals[k] = copies_of(pieces_of(given[k], held[k], CUTS), in_sems.at[k])
    own_ref, other_ref, spectrum_ref = (held[:sources] * 3)[:3]
    first_ref, last_ref, onward_ref, back_ref, bend_ref = held[sources:inputs]
    out_refs = held[inputs:]
    low_plane = z_ref[0] == 0

    for k in range(sources):
        wait_all(arrivals[k])
    extra = [pieces_taps(spectrum_ref, taps_at, own_stride)] if taps_at is not None else []
    wait_all(arrivals[sources] + arrivals[sources + 4] + arrivals[sources + 2])
    bend = bend_ref[...]
    bend_re, bend_im = bend[0], bend[1]
    leaving = []
    if taps_at is not None:
        taps = to_spectrum(extra[0], thrice(first_ref[...], 1), thrice(onward_ref[...], 0), bend) * (1.0 / LENGTH)
        out_refs[2][...] = taps
        leaving = copies_of(pieces_of(out_refs[2], results[2], 1), out_sems.at[2])
    else:
        taps = spectrum_ref[...]
    taps_re = taps[:, :LANES]
    taps_im = taps[:, LANES:]

    def gather(at):
        own, other = [], []
        for q in range(4):
            row = q * PIECE + at
            own.append(own_ref[pl.ds(own_at + row, PEERS, stride=own_stride), :])
            other.append(other_ref[pl.ds(other_at + row, PEERS, stride=other_stride), :])
        own = jnp.concatenate(own, axis=0)
        other = jnp.concatenate(other, axis=0)
        return jnp.concatenate(
            [jnp.where(low_plane, own, other), jnp.where(low_plane, other, own)], axis=0
        )

    def store(at, column):
        upper, lower = column[: ORDER // 2], column[ORDER // 2 :]
        own = jnp.where(low_plane, upper, lower)
        other = jnp.where(low_plane, lower, upper)
        for q in range(4):
            row = q * PIECE + at
            rows_own = own[q * PEERS : (q + 1) * PEERS]
            rows_other = other[q * PEERS : (q + 1) * PEERS]
            out_refs[0][pl.ds(row, PEERS, stride=BLOCK), :] = rows_own
            out_refs[1][pl.ds(row, PEERS, stride=BLOCK), :] = rows_other

    def load(channels):
        high, low = halves(jnp.concatenate([gather(at) for at in channels], axis=1))
        return jnp.concatenate([high, low, high], axis=0)

    def to_blocks(x):
        return dot(thrice(first_ref[...], 1), x)

    def bend_onward(section):
        rows = []
        for at in range(section.shape[1] // LANES):
            re = section[:ORDER, at * LANES : (at + 1) * LANES]
            im = section[ORDER:, at * LANES : (at + 1) * LANES]
            rows.append(
                jnp.concatenate([re * bend_re - im * bend_im, re * bend_im + im * bend_re], axis=1)
            )
        high, low = halves(jnp.concatenate(rows, axis=0))
        return jnp.concatenate([high, low, high], axis=1)

    def to_frequencies(x):
        return dot(x, thrice(onward_ref[...], 0))

    def weigh(spectrum):
        rows = []
        for at in range(spectrum.shape[0] // ORDER):
            re = spectrum[at * ORDER : (at + 1) * ORDER, :LANES]
            im = spectrum[at * ORDER : (at + 1) * ORDER, LANES:]
            rows.append(
                jnp.concatenate([re * taps_re - im * taps_im, re * taps_im + im * taps_re], axis=1)
            )
        high, low = halves(jnp.concatenate(rows, axis=0))
        return jnp.concatenate([high, low, high], axis=1)

    def from_frequencies(x):
        return dot(x, thrice(back_ref[...], 0))

    def bend_back(section):
        columns = []
        for at in range(section.shape[0] // ORDER):
            re = section[at * ORDER : (at + 1) * ORDER, :LANES]
            im = section[at * ORDER : (at + 1) * ORDER, LANES:]
            columns.append(
                jnp.concatenate([re * bend_re + im * bend_im, im * bend_re - re * bend_im], axis=0)
            )
        high, low = halves(jnp.concatenate(columns, axis=1))
        return jnp.concatenate([high, low, high], axis=0)

    def from_blocks(x):
        return dot(thrice(last_ref[...], 1), x)

    stages = (
        load, to_blocks, bend_onward, to_frequencies, weigh, from_frequencies, bend_back, from_blocks
    )
    batches = [tuple(range(at, at + BATCH)) for at in range(0, PIECE, BATCH)]
    state = list(batches)
    for tick in range(len(stages) + 1 + LAG * (len(batches) - 1)):
        if tick == 5:
            wait_all(arrivals[sources + 3] + arrivals[sources + 1])
        for batch, channels in enumerate(batches):
            stage = tick - LAG * batch
            if 0 <= stage < len(stages):
                state[batch] = stages[stage](state[batch])
            elif stage == len(stages):
                for at, channel in enumerate(channels):
                    store(channel, state[batch][:, at * LANES : (at + 1) * LANES])
    for k in (1, 0):
        leaving = leaving + copies_of(pieces_of(out_refs[k], results[k], CUTS), out_sems.at[k])
    wait_all(leaving)


def short_sum(short, long_ref, at, step):
    total = short[0:1] * long_ref[at + 2 : at + 2 + step, :]
    for i in range(1, TAPS):
        total = total + short[i : i + 1] * long_ref[at + 2 + i : at + 2 + i + step, :]
    return total


def fetch(proj_ref, halo_ref, short_ref, buffer_ref, halo_held, taps_held, sems, streams, columns):
    edges = copies_of([(halo_ref, halo_held), (short_ref, taps_held)], sems.at[len(columns)])
    first, count = streams
    blocks = []
    for i, column in enumerate(columns):
        lanes = pl.ds(pl.multiple_of(column, LANES), LANES)
        copy = pltpu.make_async_copy(
            proj_ref.at[pl.ds(first, count), :, lanes],
            buffer_ref.at[i, :, pl.ds(8, ROWS)],
            sems.at[i, 0],
        )
        copy.start()
        blocks.append(copy)
    wait_all(edges)
    for i, column in enumerate(columns):
        lanes = pl.ds(pl.multiple_of(column, LANES), LANES)
        buffer_ref[i, :, 0:8, :] = halo_held[first : first + count, :, lanes]
    return blocks


def feature_kernel(columns_of_z, z_ref, halo_ref, short_ref, proj_ref, *rest):
    sent_ref, product_ref = rest[-9:-7]
    buffer_ref, halo_held, taps_held, sems, out_sems, turned_ref, flat_ref = rest[-7:]
    step = 64
    columns = columns_of_z(z_ref[0])
    blocks = fetch(
        proj_ref, halo_ref, short_ref, buffer_ref, halo_held, taps_held, sems, (1, 2), columns
    )
    peers = LANES // PIECE
    leaving = []
    for i, copy in enumerate(blocks):
        copy.wait()
        lanes = pl.ds(pl.multiple_of(columns[i], LANES), LANES)
        key_taps, value_taps = taps_held[1, :, lanes], taps_held[2, :, lanes]
        for quarter in range(QUARTERS):
            parts = []
            for at in range(quarter * LANES, (quarter + 1) * LANES, step):
                product = short_sum(key_taps, buffer_ref.at[i, 0], at, step) * short_sum(
                    value_taps, buffer_ref.at[i, 1], at, step
                )
                flat_ref[i, at : at + step, :] = product
                parts.append(product)
            turned = jnp.concatenate(parts, axis=0).T
            turned_ref[i, :, quarter] = turned.reshape(peers, PIECE, LANES)
        into = sent_ref.at[
            pl.ds(i % 2 * peers, peers), pl.ds(i // 2 * QUARTERS, QUARTERS)
        ]
        pairs = [(turned_ref.at[i], into)]
        pairs.append((flat_ref.at[i], product_ref.at[:, pl.ds(i * LANES, LANES)]))
        leaving = leaving + copies_of(pairs, out_sems.at[i])
    wait_all(leaving)


def gate_kernel(chunk, z_ref, halo_ref, short_ref, proj_ref, *rest):
    gate_ref, buffer_ref, halo_held, taps_held, sems, out_sems, flat_ref = rest[-7:]
    step = 64
    columns = [(chunk * 4 + i) * LANES for i in range(4)]
    blocks = fetch(
        proj_ref, halo_ref, short_ref, buffer_ref, halo_held, taps_held, sems, (0, 1), columns
    )
    leaving = []
    for i, copy in enumerate(blocks):
        copy.wait()
        taps = taps_held[0, :, columns[i] : columns[i] + LANES]
        for at in range(0, ROWS, step):
            flat_ref[i, at : at + step, :] = short_sum(taps, buffer_ref.at[i, 0], at, step)
        pairs = [(flat_ref.at[i], gate_ref.at[:, pl.ds(i * LANES, LANES)])]
        leaving = leaving + copies_of(pairs, out_sems.at[i])
    wait_all(leaving)


def from_streams(kernel, streams, blocks, extra, out_shape, weight, z, projected, halo, short_filter, after):
    return pl.pallas_call(
        kernel,
        in_specs=[
            pl.BlockSpec(memory_space=pltpu.SMEM),
            pl.BlockSpec(memory_space=pl.ANY),
            pl.BlockSpec(memory_space=pltpu.HBM),
            pl.BlockSpec(memory_space=pltpu.HBM),
        ]
        + [pl.BlockSpec(memory_space=pl.ANY)] * len(after),
        out_specs=[pl.BlockSpec(memory_space=pl.ANY)] * len(out_shape),
        out_shape=out_shape,
        scratch_shapes=[
            pltpu.VMEM((blocks, streams, ROWS + 8, LANES), f32),
            pltpu.VMEM(halo.shape, f32),
            pltpu.VMEM(short_filter.shape, f32),
            pltpu.SemaphoreType.DMA((blocks + 1, 2)),
            pltpu.SemaphoreType.DMA((blocks, 2)),
        ]
        + extra,
        compiler_params=pltpu.CompilerParams(vmem_limit_bytes=WHOLE_BYTES),
        cost_estimate=pl.CostEstimate(
            flops=weight * 1_000_000, bytes_accessed=1_000_000, transcendentals=0
        ),
        name="streams",
    )(z, halo, short_filter, projected, *after)


def features_of(z, parts, projected, halo, short_filter, after=(), weight=1):
    blocks = 2 * len(parts)

    def columns_of_z(plane):
        firsts = [chunk * 4 + (1 - plane if slot else plane) * 2 for chunk, slot in parts]
        return [(firsts[i // 2] + i % 2) * LANES for i in range(blocks)]

    out_shape = [
        jax.ShapeDtypeStruct((PEERS, len(parts) * QUARTERS, PIECE, LANES), f32),
        jax.ShapeDtypeStruct((ROWS, blocks * LANES), f32),
    ]
    kernel = functools.partial(feature_kernel, columns_of_z)
    extra = [
        pltpu.VMEM((blocks, LANES // PIECE, QUARTERS, PIECE, LANES), f32),
        pltpu.VMEM((blocks, ROWS, LANES), f32),
    ]
    return from_streams(
        kernel, 2, blocks, extra, out_shape, weight, z, projected, halo, short_filter, after
    )


def gates_of(z, chunk, projected, halo, short_filter, after):
    out_shape = [jax.ShapeDtypeStruct((ROWS, 4 * LANES), f32)]
    kernel = functools.partial(gate_kernel, chunk)
    extra = [pltpu.VMEM((4, ROWS, LANES), f32)]
    return from_streams(
        kernel, 1, 4, extra, out_shape, SLOW, z, projected, halo, short_filter, after
    )[0]


def finish_kernel(
    z_ref,
    out_part_ref,
    b_ref,
    gate_a_ref,
    gate_b_ref,
    own_ref,
    a_product_ref,
    b_product_ref,
    skip_ref,
    out_ref,
    long_vmem,
    own_vmem,
    out_vmem,
    in_sems,
    out_sems,
):
    z = z_ref[0]
    wide = 2 * LANES
    places, products, gates = [], [], []
    arrivals = []
    for i in range(4):
        plane = 1 - z if i % 2 else z
        column = pl.multiple_of((i // 2 * 4 + plane * 2) * LANES, wide)
        lanes = pl.ds(column, wide)
        places.append(lanes)
        half = pl.ds(pl.multiple_of(plane * wide, wide), wide)
        if i % 2:
            products.append((a_product_ref, slice(0, wide)) if i < 2 else (b_product_ref, slice(0, wide)))
        else:
            products.append((own_vmem.at[i // 2], slice(0, wide)))
        gates.append(((gate_a_ref, gate_b_ref)[i // 2], half))
        long = out_part_ref.at[:, pl.ds(QUARTERS * i, QUARTERS)] if i < 3 else b_ref
        pairs = [(long, long_vmem.at[i])]
        if i % 2 == 0:
            own = own_ref.at[:, pl.ds(i // 2 * wide, wide)]
            pairs.append((own, own_vmem.at[i // 2]))
        arrivals.append(copies_of(pairs, in_sems.at[i]))
    leaving = []
    for i in range(4):
        wait_all(arrivals[i])
        skip = skip_ref[0:1, places[i]]
        for quarter in range(QUARTERS):
            rows = slice(quarter * LANES, (quarter + 1) * LANES)
            turned = long_vmem[i, :, quarter].reshape(wide, LANES).T
            gate, half = gates[i]
            product, lanes = products[i]
            out_vmem[i, rows, :] = gate[rows, half] * (turned + skip * product[rows, lanes])
        leaving = leaving + copies_of(
            [(out_vmem.at[i], out_ref.at[:, places[i]])], out_sems.at[i]
        )
    wait_all(leaving)


def finish(z, out_part, b_back, gate_a, gate_b, product_own, product_a, product_b, skip):
    anywhere = pl.BlockSpec(memory_space=pl.ANY)
    flat = pltpu.VMEM((4, ROWS, 2 * LANES), f32)
    return pl.pallas_call(
        finish_kernel,
        in_specs=[pl.BlockSpec(memory_space=pltpu.SMEM)]
        + [anywhere] * 2
        + [pl.BlockSpec(memory_space=pltpu.VMEM)] * 2
        + [anywhere]
        + [pl.BlockSpec(memory_space=pltpu.VMEM)] * 3,
        out_specs=anywhere,
        out_shape=jax.ShapeDtypeStruct((ROWS, 8 * LANES), f32),
        scratch_shapes=[
            pltpu.VMEM((4, PEERS, QUARTERS, PIECE, LANES), f32),
            pltpu.VMEM((2, ROWS, 2 * LANES), f32),
            flat,
            pltpu.SemaphoreType.DMA((4, 2)),
            pltpu.SemaphoreType.DMA((4, 1)),
        ],
        compiler_params=pltpu.CompilerParams(vmem_limit_bytes=CONV_BYTES),
        cost_estimate=pl.CostEstimate(
            flops=1_000_000, bytes_accessed=1_000_000, transcendentals=0
        ),
        name="finish",
    )(z, out_part, b_back, gate_a, gate_b, product_own, product_a, product_b, skip)


def convolve(z, layout, sources, tables, after=()):
    out_shape = [jax.ShapeDtypeStruct((HALF, LANES), f32)] * 2
    if layout[-1] is not None:
        out_shape = out_shape + [jax.ShapeDtypeStruct((ORDER, 2 * LANES), f32)]
    operands = list(sources) + [
        in_hbm(tables[name]) for name in ("first", "last", "onward", "back", "bend")
    ]
    anywhere = pl.BlockSpec(memory_space=pl.ANY)
    shapes = [(x.shape, x.dtype) for x in operands + out_shape]
    return pl.pallas_call(
        functools.partial(conv_kernel, layout, len(sources), len(out_shape), len(after)),
        in_specs=[pl.BlockSpec(memory_space=pltpu.SMEM)]
        + [anywhere] * (len(operands) + len(after)),
        out_specs=[anywhere] * len(out_shape),
        out_shape=out_shape,
        scratch_shapes=[pltpu.VMEM(shape, dtype) for shape, dtype in shapes]
        + [
            pltpu.SemaphoreType.DMA((len(operands), CUTS)),
            pltpu.SemaphoreType.DMA((len(out_shape), CUTS)),
        ],
        compiler_params=pltpu.CompilerParams(vmem_limit_bytes=WHOLE_BYTES),
        cost_estimate=pl.CostEstimate(
            flops=10_000_000, bytes_accessed=1_000_000, transcendentals=0
        ),
        name="convolve",
    )(z, *operands, *after)


def in_hbm(x):
    return pltpu.with_memory_space_constraint(x, pltpu.HBM)


def swap_planes(x):
    return lax.ppermute(x, "zh", [(0, 1), (1, 0)])


def across(x):
    return lax.all_to_all(x, PLANE, split_axis=0, concat_axis=0, tiled=True)


def relay(pairs, held_refs, in_sems, out_sems):
    arrivals, targets = [], []
    for at, ((source, target), held) in enumerate(zip(pairs, held_refs)):
        arrivals.append(copies_of(pieces_of(source, held, CUTS), in_sems.at[at]))
        targets.append(pieces_of(held, target, CUTS))
    leaving = []
    for cut in range(CUTS):
        for at in range(len(pairs)):
            arrivals[at][cut].wait()
            source, target = targets[at][cut]
            copy = pltpu.make_async_copy(source, target, out_sems.at[at, cut])
            copy.start()
            leaving.append(copy)
    return leaving


def join_taps_kernel(
    place_ref,
    own_ref,
    from_ref,
    here_ref,
    there_ref,
    out_ref,
    own_held,
    from_held,
    in_sems,
    out_sems,
    taps_held,
    small_held,
    small_sems,
):
    pairs = [
        (own_ref, out_ref.at[:, pl.ds(0, 2 * QUARTERS)]),
        (from_ref, out_ref.at[:, pl.ds(2 * QUARTERS, QUARTERS)]),
    ]
    small = [(here_ref, small_held.at[0]), (there_ref, small_held.at[1])]
    wait_all(copies_of(small, small_sems))
    leaving = relay(pairs, (own_held, from_held), in_sems, out_sems)
    z, group = place_ref[0], place_ref[1]
    for zq in range(8):
        row = (jnp.bitwise_xor(zq % 4, group) * 4) + group
        here = small_held[0, pl.ds(row, 1), :]
        there = small_held[1, pl.ds(row, 1), :]
        taps = jnp.where(z == zq // 4, here, there)
        taps_held[:, 0, zq : zq + 1, :] = jnp.broadcast_to(taps[None], (PEERS, 1, LANES))
    into = out_ref.at[:, pl.ds(3 * QUARTERS, 1)]
    wait_all(leaving + copies_of([(taps_held, into)], small_sems))


def join_kernel(a_ref, from_ref, b_ref, out_ref, a_held, from_held, b_held, in_sems, out_sems):
    pairs = [
        (ref, out_ref.at[:, pl.ds(QUARTERS * at, QUARTERS)])
        for at, ref in enumerate((a_ref, from_ref, b_ref))
    ]
    wait_all(relay(pairs, (a_held, from_held, b_held), in_sems, out_sems))


def rearrange(kernel, operands, groups, pieces, place=None, cost=10_000_000_000):
    anywhere = pl.BlockSpec(memory_space=pl.ANY)
    scratch = [pltpu.VMEM(x.shape, f32) for x in operands[:pieces]]
    scratch = scratch + [pltpu.SemaphoreType.DMA((pieces, CUTS))] * 2
    in_specs = [anywhere] * len(operands)
    if place is not None:
        scratch.append(pltpu.VMEM((PEERS, 1, PIECE, LANES), f32))
        scratch.append(pltpu.VMEM((2, 16, LANES), f32))
        scratch.append(pltpu.SemaphoreType.DMA((2,)))
        in_specs = [pl.BlockSpec(memory_space=pltpu.SMEM)] + in_specs
        operands = (place, *operands)
    return pl.pallas_call(
        kernel,
        in_specs=in_specs,
        out_specs=anywhere,
        out_shape=jax.ShapeDtypeStruct((PEERS, groups, PIECE, LANES), f32),
        scratch_shapes=scratch,
        compiler_params=pltpu.CompilerParams(vmem_limit_bytes=VMEM_BYTES),
        cost_estimate=pl.CostEstimate(flops=cost, bytes_accessed=1_000, transcendentals=0),
        name="rearrange",
    )(*operands)


def later_kernel(*refs):
    for at in range(4):
        refs[-1][at * 4 : (at + 1) * 4] = refs[at][...]


def later_rows(parts, after):
    inside = pl.BlockSpec(memory_space=pltpu.VMEM)
    return pl.pallas_call(
        later_kernel,
        in_specs=[inside] * 4 + [pl.BlockSpec(memory_space=pl.ANY)],
        out_specs=inside,
        out_shape=jax.ShapeDtypeStruct((16, LANES), f32),
        cost_estimate=pl.CostEstimate(flops=1_000, bytes_accessed=1_000, transcendentals=0),
        name="later",
    )(*parts, after)


def body(projected, short_filter, long_filter, skip_gain):
    tables = {name: jnp.asarray(table) for name, table in make_tables().items()}
    z = lax.axis_index("zh").astype(jnp.int32).reshape(1)
    skip = skip_gain.reshape(1, -1)
    devices = lax.axis_size(SEQ)
    halo = lax.ppermute(
        projected[:, ROWS - 8 :, :], SEQ, [(i, i + 1) for i in range(devices - 1)]
    )
    projected, short_filter = in_hbm(projected), in_hbm(short_filter)
    feature = functools.partial(
        features_of, projected=projected, halo=halo, short_filter=short_filter
    )
    a_other, product_a = feature(z, ((0, 1),))
    a_from = swap_planes(a_other)
    b_other, product_b = feature(z, ((1, 1),), after=(product_a,))
    b_there = across(b_other)
    own, product_own = feature(z, ((0, 0), (1, 0)), after=(product_b,), weight=SLOW)

    steps = [
        lax.ppermute(long_filter, "zl", [(i, i ^ d) for i in range(4)]) for d in range(1, 4)
    ]
    taps_here = later_rows((long_filter, *steps), own)
    taps_there = swap_planes(taps_here)
    group = lax.axis_index("zl").astype(jnp.int32).reshape(1)
    place = jnp.concatenate([z, group])

    b_from = swap_planes(b_there)
    sent = rearrange(
        join_taps_kernel,
        (in_hbm(own), a_from, taps_here, taps_there),
        3 * QUARTERS + 1,
        2,
        place=place,
    )
    here = across(sent).reshape(-1, LANES)
    gate_a = gates_of(z, 0, projected, halo, short_filter, (a_from, b_there))
    wide = 3 * BLOCK + 8
    conv_a_own, conv_a_other, spectrum = convolve(
        z, (0, wide, 2 * BLOCK, wide, 3 * BLOCK), (in_hbm(here),), tables, (gate_a,)
    )

    pieces = (PEERS, QUARTERS, PIECE, LANES)
    a_back = swap_planes(conv_a_other.reshape(pieces))
    conv_b_own, conv_b_other = convolve(
        z,
        (BLOCK, wide, 0, BLOCK, None),
        (in_hbm(here), b_from.reshape(HALF, LANES), spectrum),
        tables,
    )
    b_out = across(conv_b_other.reshape(pieces))

    b_back = swap_planes(b_out)
    gate_b = gates_of(z, 1, projected, halo, short_filter, (a_back, b_out))
    sent = rearrange(
        join_kernel,
        (in_hbm(conv_a_own.reshape(pieces)), a_back, in_hbm(conv_b_own.reshape(pieces))),
        3 * QUARTERS,
        3,
    )
    out_part = across(sent)
    return finish(
        z,
        out_part,
        b_back,
        gate_a,
        gate_b,
        in_hbm(product_own),
        product_a,
        product_b,
        skip,
    )


def solution(mesh):
    fine = Mesh(mesh.devices.reshape(4, 2, 4, 2, 4), ("x", "zh", "y", "core", "zl"))
    placed = (P(None, SEQ, "zl"), P(None, None, "zl"), P(None, SEQ + ("zl",)), P("zl"))
    return jax.shard_map(
        body, mesh=fine, in_specs=placed, out_specs=P(SEQ, "zl"), check_vma=False
    )
```
